256 devices in a mesh: fsdp: 64 (over z, y, core), tp: 4 (over x).
Axes of the slice: x: 4, y: 4, z: 8, core: 2. Of those that a mesh axis runs over, the one named last changes fastest.
Arguments:
- momentum: float32 [8192, 26624], P('fsdp', 'tp'), may hold values from -12 to 12
- gradient: bfloat16 [8192, 26624], P('fsdp', 'tp'), may hold values from -16 to 16
- right_prior: bfloat16 [4, 6656, 512], P('tp', 'fsdp'), may hold values from -0.0390625 to 0.0390625
Outputs:
- momentum_next: float32 [8192, 26624], P('fsdp', 'tp')
- update: bfloat16 [8192, 26624], P('fsdp', 'tp')
- right_next: bfloat16 [4, 6656, 512], P('tp', 'fsdp')
The draws below stay inside these ranges and needn't reach their ends.
All inputs are finite; a program needn't handle non-finite values.
Results may differ from the reference program's by a relative error of at most 0.009.
Values may be sent and summed in bfloat16 or wider, within the bound.
A program may use at most 128 MiB of HBM per device.

```python
import math
import jax
import jax.numpy as jnp
from jax import lax

COLS = 26624
RANK = 512
ROWS = 8192
N_TP = 4


def column_ramp(top):
    group = COLS // N_TP
    position = jnp.arange(COLS, dtype=jnp.int32) % group
    fraction = position.astype(jnp.float32) / float(max(group - 1, 1))
    return 1.0 + (top - 1.0) * fraction


def draw_momentum(key, part):
    key = jax.random.fold_in(key, 11)
    factors = max(RANK // 4, 2)
    subkeys = jax.random.split(key, 4)
    strengths = jnp.exp(jax.random.uniform(subkeys[0], (factors,), jnp.float32, math.log(0.5), math.log(2.0)))
    background = jax.random.normal(subkeys[3], (ROWS, COLS), jnp.float32)
    ramp = column_ramp(2.5)
    left_part = jax.random.normal(subkeys[1], (ROWS, factors), jnp.float32) * (strengths / math.sqrt(factors))
    right_part = jax.random.normal(subkeys[2], (factors, COLS), jnp.float32)
    low_rank = jnp.dot(left_part, right_part, precision=lax.Precision.HIGHEST)
    return jnp.clip((low_rank + background) * ramp, -12.0, 12.0)


def raised(drawn, own_key, source, target, blocks, factor):
    owner, partner = [(jnp.arange(drawn.shape[dim]) // (drawn.shape[dim] // blocks)).reshape([-1 if axis == dim else 1 for axis in range(drawn.ndim)]) for dim in (source, target)]
    chosen = jax.random.permutation(own_key, blocks)[partner]
    strong = (owner == chosen) | (owner == (partner + blocks // 2) % blocks)
    return jnp.where(strong, factor * drawn, drawn)


def steps_of(stream_key, dims, pieces, low, top_value):
    def one(dim, shards_of):
        draws = jax.random.uniform(jax.random.fold_in(jax.random.fold_in(stream_key, 6), dim), (shards_of,), jnp.float32, low / len(pieces), top_value / len(pieces))
        return jnp.repeat(jnp.exp(draws), dims[dim] // shards_of).reshape((-1,) + (1,) * (len(dims) - dim - 1))

    level = one(*pieces[0])
    for cut in pieces[1:]:
        level = level * one(*cut)
    return level


def noise(rng, shape, width, reach, cuts=(), kind=jnp.bfloat16):
    drawn = jax.random.normal(rng, shape, jnp.float32) * width
    if len(cuts) > 0:
        drawn = steps_of(rng, shape, cuts, -0.22, 0.18) * drawn
    return jnp.clip(drawn, min=-reach, max=reach).astype(kind)


def bell_draw_with(own_key, extent, deviation, reach, pieces, heavy, kind=jnp.bfloat16):
    values = deviation * jax.random.normal(own_key, extent, jnp.float32)
    if pieces:
        values = values * steps_of(own_key, extent, pieces, -0.22, 0.18)
    return jnp.clip(raised(values, jax.random.fold_in(own_key, 3), *heavy), -reach, reach).astype(kind)


def setup_inputs(seed: int = 0) -> dict:
    arg_keys = jax.random.split(jax.random.key(seed), 4)
    return {
        "momentum": draw_momentum(jax.random.fold_in(arg_keys[3], 71), 0),
        "gradient": bell_draw_with(arg_keys[1], (ROWS, COLS), 1.0, 16.0, ((0, 64), (1, 4)), (0, 1, 64, 4.0)),
        "right_prior": noise(arg_keys[2], (N_TP, COLS // N_TP, RANK), COLS ** -0.5, 0.0390625, ((0, 4), (1, 64))),
    }


def reference(momentum, gradient, right_prior):
    decay = 0.95
    prior = right_prior.reshape(COLS, RANK)
    blended = momentum + gradient.astype(jnp.float32)
    blend_half = blended.astype(jnp.bfloat16)
    left_factor = jnp.dot(blend_half.astype(jnp.float32), prior.astype(jnp.float32), preferred_element_type=jnp.float32)
    gram_matrix = jnp.dot(left_factor.T, left_factor, precision=lax.Precision.HIGHEST)
    lower = jnp.linalg.cholesky(gram_matrix)
    orthonormal = lax.linalg.triangular_solve(lower, left_factor, left_side=False, lower=True, transpose_a=True)
    ortho_half = orthonormal.astype(jnp.bfloat16)
    right_full = jnp.dot(blend_half.T.astype(jnp.float32), ortho_half.astype(jnp.float32), preferred_element_type=jnp.float32)
    right_half = right_full.astype(jnp.bfloat16)
    column_scale = 1.0 / jnp.sqrt(lax.optimization_barrier(jnp.sum(right_full * right_full, axis=0)) + 1e-06)
    right_next = (right_full * column_scale).astype(jnp.bfloat16).reshape(N_TP, COLS // N_TP, RANK)
    momentum_next = blended - (1.0 - decay) * jnp.dot(ortho_half.astype(jnp.float32), right_half.T.astype(jnp.float32), preferred_element_type=jnp.float32)
    magnitude = math.sqrt(ROWS * COLS / RANK)
    update_left = (orthonormal * column_scale * magnitude).astype(jnp.bfloat16)
    update = jnp.dot(update_left.astype(jnp.float32), right_half.T.astype(jnp.float32), preferred_element_type=jnp.float32).astype(jnp.bfloat16)
    return (momentum_next, update, right_next)
```

```python
import functools
import math

import jax
import jax.numpy as jnp
from jax import lax
from jax.experimental import pallas as pl
from jax.experimental.pallas import tpu as pltpu
from jax.sharding import PartitionSpec as P

HIGHEST = lax.Precision.HIGHEST
MESH = pl.DeviceIdType.MESH
F32 = jnp.float32
BF16 = jnp.bfloat16
VMEM_SPEC = pl.BlockSpec(memory_space=pltpu.VMEM)
VMEM_LIMIT = 60 * 1024 * 1024
BLOCK = 128
Y_CHIPS = 4


def wrap(value, size):
    return lax.rem(value + size, size)


def exact_dot(a, b, a_dim, b_dim):
    return lax.dot_general(
        a, b, (((a_dim,), (b_dim,)), ((), ())), precision=HIGHEST, preferred_element_type=F32
    )


class Place:
    def __init__(self, nz, ny, nx):
        self.nz, self.ny, self.nx = nz, ny, nx
        index = lax.axis_index("fsdp")
        self.x = lax.axis_index("tp")
        self.core = lax.rem(index, 2)
        self.y = lax.rem(lax.div(index, 2), ny)
        self.z = lax.div(index, 2 * ny)

    def device(self, z=None, y=None, core=None, x=None):
        z = self.z if z is None else z
        y = self.y if y is None else y
        core = self.core if core is None else core
        x = self.x if x is None else x
        return ((z * self.ny + y) * 2 + core, x)

    def partner(self):
        return self.device(core=1 - self.core)

    def x_peers(self):
        return [self.device(x=wrap(self.x + o, self.nx)) for o in range(1, self.nx)]

    def y_peers(self):
        return [self.device(y=wrap(self.y + o, self.ny)) for o in range(1, self.ny)]

    def z_peers(self):
        return [self.device(z=wrap(self.z + o, self.nz)) for o in range(1, self.nz)]

    def neighbours(self):
        return [
            self.device(z=wrap(self.z + 1, self.nz)),
            self.device(z=wrap(self.z + self.nz - 1, self.nz)),
            self.device(y=wrap(self.y + 1, self.ny)),
            self.device(y=wrap(self.y + self.ny - 1, self.ny)),
        ]

    def chip(self):
        return self.z * self.ny + self.y


def greet(devices):
    barrier = pltpu.get_barrier_semaphore()
    for device in devices:
        pl.semaphore_signal(barrier, inc=1, device_id=device, device_id_type=MESH)
    pl.semaphore_wait(barrier, len(devices))


def remote(src, dst, send_sem, recv_sem, device):
    return pltpu.make_async_remote_copy(
        src_ref=src, dst_ref=dst, send_sem=send_sem, recv_sem=recv_sem,
        device_id=device, device_id_type=MESH,
    )


def halves(rows, unit):
    first = -(-(rows // 2) // unit) * unit
    return ((0, first), (first, rows - first))


def gather_plane(buf, rows, na, nb, me_a, me_b, slot, device, ssem, rsem, done=None, extras=()):
    spans = halves(rows, 16)
    half_a, half_b = na // 2, nb // 2

    def piece(a, b, part):
        offset, size = (0, rows) if part is None else spans[part]
        start = pl.multiple_of(slot(a, b) * rows + offset, 16)
        return buf.at[pl.ds(start, size), :]

    def copy(key, sending):
        kind, d, step, ra = key
        sign = 1 - 2 * d
        back = step - 1 if sending else step
        if kind == 0:
            part = d if step == half_a else None
            a, b = wrap(me_a - sign * back, na), me_b
            target = device(wrap(me_a + sign, na), me_b)
            index = d * half_a + step - 1
        else:
            part = d if step == half_b else None
            a, b = wrap(me_a + ra, na), wrap(me_b - sign * back, nb)
            target = device(me_a, wrap(me_b + sign, nb))
            index = na + (d * half_b + step - 1) * na + ra
        ref = piece(a, b, part)
        return remote(ref, ref, ssem.at[index], rsem.at[index], target)

    started = []

    def start(key):
        copy(key, True).start()
        started.append(key)

    def spread(ra):
        for d in (0, 1):
            start((1, d, 1, ra))

    def finish(ra, b):
        if done is not None:
            done(slot(wrap(me_a + ra, na), b))

    for d in (0, 1):
        start((0, d, 1, 0))
    spread(0)
    finish(0, me_b)
    events = []
    for step in range(1, half_a + 1):
        for d in (0, 1):
            events.append((step, 0, d, step, 0))
    for step in range(1, half_b + 1):
        for ra in range(na):
            for d in (0, 1):
                events.append((min(ra, na - ra) + step, 1, min(ra, na - ra), ra, d, step))
    events.sort()
    landed = {}
    extras = list(extras)
    gap = max(1, len(events) // (len(extras) + 1))
    for count, event in enumerate(events):
        if event[1] == 0:
            _, _, d, step, _ = event
            sign = 1 - 2 * d
            copy((0, d, step, 0), False).wait_recv()
            if step < half_a:
                start((0, d, step + 1, 0))
                ra = (-sign * step) % na
                spread(ra)
                finish(ra, me_b)
            else:
                landed["a"] = landed.get("a", 0) + 1
                if landed["a"] == 2:
                    spread(half_a)
                    finish(half_a, me_b)
        else:
            _, _, _, ra, d, step = event
            sign = 1 - 2 * d
            copy((1, d, step, ra), False).wait_recv()
            if step < half_b:
                start((1, d, step + 1, ra))
                finish(ra, wrap(me_b - sign * step, nb))
            else:
                landed[ra] = landed.get(ra, 0) + 1
                if landed[ra] == 2:
                    finish(ra, wrap(me_b + half_b, nb))
        if extras and (count + 1) % gap == 0:
            extras.pop(0)()
    for extra in extras:
        extra()
    for key in started:
        copy(key, True).wait_send()


def reduce_ring(total, inbox, rows, n, me, order, chunk, device, ssem, rsem, base):
    spans = halves(rows, 8)
    half = n // 2
    count = len(order)

    def index(d, step, j):
        return base + (d * half + step - 1) * count + j

    def span(part):
        return (0, rows) if part is None else spans[part]

    def rows_at(dest, j, part):
        offset, size = span(part)
        return pl.ds(pl.multiple_of(chunk(dest, j) + offset, 8), size)

    def landing(d, step, j, part):
        offset, size = span(part)
        return inbox.at[index(d, step, j), pl.ds(offset, size), :]

    def copy(d, step, j):
        sign = 1 - 2 * d
        part = d if step == 1 else None
        if step == 1:
            src = total.at[rows_at(wrap(me - sign * half, n), j, part), :]
        else:
            src = landing(d, step - 1, j, part)
        i = index(d, step, j)
        return remote(src, landing(d, step, j, part), ssem.at[i], rsem.at[i], device(wrap(me - sign, n)))

    for j in order:
        for d in (0, 1):
            copy(d, 1, j).start()
    yield
    for step in range(1, half + 1):
        for j in order:
            for d in (0, 1):
                sign = 1 - 2 * d
                copy(d, step, j).wait_recv()
                if step < half:
                    dest = wrap(me - sign * (half - step), n)
                    for part in (0, 1):
                        here = landing(d, step, j, part)
                        own = total[rows_at(dest, j, part), :]
                        if step == 1 and part != d:
                            here[...] = own
                        else:
                            here[...] = here[...] + own
                    copy(d, step + 1, j).start()
                else:
                    part = d if step == 1 else None
                    own = rows_at(me, j, part)
                    total[own, :] = total[own, :] + landing(d, step, j, part)[...]
        yield
    for step in range(1, half + 1):
        for j in order:
            for d in (0, 1):
                copy(d, step, j).wait_send()


def far_first(n):
    return sorted(range(n), key=lambda j: (-min(j, n - j), j))


def reduce_plane(total, inbox_a, inbox_b, rows, na, nb, me_a, me_b, slot, device, ssem, rsem):
    order = far_first(nb)
    yield from reduce_ring(
        total, inbox_a, rows, na, me_a, order,
        lambda dest, j: slot(dest, wrap(me_b + j, nb)) * rows,
        lambda a: device(a, me_b), ssem, rsem, 0,
    )
    used = na * nb
    yield from reduce_ring(
        total, inbox_b, rows, nb, me_b, [0],
        lambda dest, j: slot(me_a, dest) * rows,
        lambda b: device(me_a, b), ssem.at[pl.ds(used, nb)], rsem.at[pl.ds(used, nb)], 0,
    )


def column_first(place):
    return dict(
        na=place.nz, nb=place.ny, me_a=place.z, me_b=place.y,
        slot=lambda a, b: a * place.ny + b,
        device=lambda a, b: place.device(z=a, y=b),
    )


def row_first(place):
    return dict(
        na=place.ny, nb=place.nz, me_a=place.y, me_b=place.z,
        slot=lambda a, b: b * place.ny + a,
        device=lambda a, b: place.device(z=b, y=a),
    )


def run_all(steps):
    for _ in steps:
        pass


def rows_of(tile, k):
    return jnp.broadcast_to(tile[k : k + 1, :], tile.shape)


def columns_of(tile, k):
    return jnp.broadcast_to(tile[:, k : k + 1], tile.shape)


def inverse_factor(block):
    count = BLOCK // 8
    d = [block[8 * i : 8 * i + 8, :] for i in range(count)]
    row = lax.broadcasted_iota(jnp.int32, (8, BLOCK), 0)
    lane = lax.broadcasted_iota(jnp.int32, (8, BLOCK), 1)
    e = [(row + 8 * i == lane).astype(F32) for i in range(count)]
    out = []
    for s in range(count):
        c = [[columns_of(d[i], 8 * s + k) for k in range(8)] for i in range(s, count)]
        pivots = jnp.zeros((8, BLOCK), F32)
        for k in range(8):
            pivot = rows_of(c[0][k], k)
            inverse = 1.0 / pivot
            pivots = jnp.where(row == k, pivot, pivots)
            d_row, e_row = rows_of(d[s], k), rows_of(e[s], k)
            later = [rows_of(c[0][q], k) for q in range(k + 1, 8)]
            for i in range(s, count):
                factor = c[i - s][k] * inverse
                if i == s:
                    factor = jnp.where(row > k, factor, 0.0)
                d[i] = d[i] - factor * d_row
                e[i] = e[i] - factor * e_row
                for q in range(k + 1, 8):
                    c[i - s][q] = c[i - s][q] - factor * later[q - k - 1]
        out.append(e[s] * lax.rsqrt(pivots))
    return jnp.concatenate(out, axis=0)


def factor_steps(a, w):
    size = a.shape[0]
    w[...] = jnp.zeros((size, size), F32)
    for o in range(0, size, BLOCK):
        end = o + BLOCK
        inverse = inverse_factor(a[o:end, o:end])
        w[o:end, o:end] = inverse
        if end < size:
            low = exact_dot(a[end:, o:end], inverse, 1, 1)
            a[end:, o:end] = low
            a[end:, end:] = a[end:, end:] - exact_dot(low, low, 1, 1)
        if o:
            through = exact_dot(a[o:end, :o], w[:o, :o], 1, 0)
            w[o:end, :o] = -exact_dot(inverse, through, 1, 0)
        yield
def left_kernel(dims, blend, prior, left, pair, mine, given, buf, partial, inbox,
                swap_send, swap_recv, keep_sem, ring_send, ring_recv, x_send, x_recv):
    place = Place(*dims)
    core, partner = place.core, place.partner()
    shard, rank = prior.shape
    half = rank // 2
    rows, columns = blend.shape
    peers = place.x_peers()
    greet([partner] + peers + place.neighbours())

    low, high = prior[:, :half].astype(F32), prior[:, half:].astype(F32)
    given[...] = jnp.where(core == 0, high, low)
    at_mine = mine.at[pl.ds(pl.multiple_of(core * shard, 8), shard), :]
    swap = remote(given, at_mine, swap_send.at[0], swap_recv.at[0], partner)
    swap.start()
    swap_blend = remote(blend, pair.at[core], swap_send.at[1], swap_recv.at[1], partner)
    swap_blend.start()
    keep = pltpu.make_async_copy(blend, pair.at[core], keep_sem)
    keep.start()
    at_mine[...] = jnp.where(core == 0, low, high)
    swap.wait_recv()
    piece = 2 * shard
    buf[pl.ds(pl.multiple_of(place.chip() * piece, 16), piece), :] = mine[...].astype(BF16)

    @pl.when(core == 0)
    def _():
        gather_plane(buf, piece, ssem=ring_send, rsem=ring_recv, **column_first(place))

    @pl.when(core == 1)
    def _():
        gather_plane(buf, piece, ssem=ring_send, rsem=ring_recv, **row_first(place))

    keep.wait()
    swap_blend.wait_recv()
    width = 1664 if columns % 1664 == 0 else BLOCK
    partial[...] = jnp.zeros_like(partial)

    @pl.loop(0, columns // width)
    def _(i):
        at = pl.ds(pl.multiple_of(i * width, BLOCK), width)
        for c in range(2):
            own = slice(c * rows, (c + 1) * rows)
            partial[own, :] += jnp.dot(pair[c, :, at], buf[at, :], preferred_element_type=F32)

    part = 2 * rows // place.nx
    at_x = lambda x: pl.ds(pl.multiple_of(x * part, 8), part)
    copies = []
    for o, peer in enumerate(peers, 1):
        copies.append(remote(partial.at[at_x(wrap(place.x + o, place.nx)), :], inbox.at[o],
                             x_send.at[o], x_recv.at[o], peer))
        copies[-1].start()
    total = partial[at_x(place.x), :]
    for o, copy in enumerate(copies, 1):
        copy.wait_recv()
        total = total + inbox[o]
    left[at_x(place.x), :] = total
    for o, peer in enumerate(peers, 1):
        here = left.at[at_x(place.x), :]
        copies.append(remote(here, here, x_send.at[place.nx + o], x_recv.at[place.nx + o], peer))
        copies[-1].start()
    for o in range(1, place.nx):
        there = left.at[at_x(wrap(place.x - o, place.nx)), :]
        remote(there, there, x_send.at[place.nx + o], x_recv.at[place.nx + o], peers[o - 1]).wait_recv()
    for copy in copies + [swap, swap_blend]:
        copy.wait_send()


def left_factor_call(dims, blend, prior):
    nz, ny, nx = dims
    shard, rank = prior.shape
    rows, columns = blend.shape
    half = rank // 2
    ring = nz * ny + max(nz, ny)
    dma = pltpu.SemaphoreType.DMA
    return pl.pallas_call(
        functools.partial(left_kernel, dims),
        out_shape=(
            jax.ShapeDtypeStruct((2 * rows, half), F32),
            jax.ShapeDtypeStruct((2, rows, columns), BF16),
        ),
        in_specs=[VMEM_SPEC] * 2,
        out_specs=(VMEM_SPEC,) * 2,
        scratch_shapes=[
            pltpu.VMEM((2 * shard, half), F32),
            pltpu.VMEM((shard, half), F32),
            pltpu.VMEM((columns, half), BF16),
            pltpu.VMEM((2 * rows, half), F32),
            pltpu.VMEM((nx, 2 * rows // nx, half), F32),
            dma((2,)), dma((2,)), dma, dma((ring,)), dma((ring,)), dma((2 * nx,)), dma((2 * nx,)),
        ],
        compiler_params=pltpu.CompilerParams(
            collective_id=0, has_side_effects=True, vmem_limit_bytes=VMEM_LIMIT
        ),
        name="left_factor",
    )(blend, prior)


def gram_steps(place, left, both, part, z_in, y_in, gram, send, recv):
    core, partner = place.core, place.partner()
    nz, ny, nx = place.nz, place.ny, place.nx
    half = left.shape[1]
    across = 2 * half // nx
    rows = across // nz
    base = [0]

    def sems(count):
        base[0] += count
        return base[0] - count

    sent = []

    def start(src, dst, index, device):
        copy = remote(src, dst, send.at[index], recv.at[index], device)
        copy.start()
        sent.append(copy)
        return copy

    def wait(ref, index, device):
        remote(ref, ref, send.at[index], recv.at[index], device).wait_recv()

    i = sems(1)
    start(left, both.at[core], i, partner)
    both[core] = left[...]
    wait(both.at[1 - core], i, partner)
    per = half // across
    block = both[lax.div(place.x, per), :, pl.ds(pl.multiple_of(lax.rem(place.x, per) * across, BLOCK), across)]
    part[...] = exact_dot(block, left[...], 0, 0)

    z_peers, y_peers, x_peers = place.z_peers(), place.y_peers(), place.x_peers()
    at_z = lambda z: pl.ds(pl.multiple_of(z * rows, 8), rows)
    i = sems(nz)
    for o, peer in enumerate(z_peers, 1):
        start(part.at[at_z(wrap(place.z + o, nz)), :], z_in.at[o], i + o, peer)
    total = part[at_z(place.z), :]
    for o, peer in enumerate(z_peers, 1):
        wait(z_in.at[o], i + o, peer)
        total = total + z_in[o]
    i = sems(ny)
    y_in[place.y] = total
    for o, peer in enumerate(y_peers, 1):
        start(y_in.at[place.y], y_in.at[place.y], i + o, peer)
    for o, peer in enumerate(y_peers, 1):
        wait(y_in.at[wrap(place.y - o, ny)], i + o, peer)
    total = y_in[0]
    for y in range(1, ny):
        total = total + y_in[y]

    def at(x, z):
        return gram.at[core, pl.ds(pl.multiple_of(x * across + z * rows, 8), rows), :]

    at(place.x, place.z)[...] = total
    i = sems(nz)
    for o, peer in enumerate(z_peers, 1):
        start(at(place.x, place.z), at(place.x, place.z), i + o, peer)
    for o, peer in enumerate(z_peers, 1):
        wait(at(place.x, wrap(place.z - o, nz)), i + o, peer)
    whole = lambda x: gram.at[core, pl.ds(pl.multiple_of(x * across, 8), across), :]
    i = sems(nx)
    for o, peer in enumerate(x_peers, 1):
        start(whole(place.x), whole(place.x), i + o, peer)
    for o, peer in enumerate(x_peers, 1):
        wait(whole(wrap(place.x - o, nx)), i + o, peer)
    i = sems(1)
    start(gram.at[core], gram.at[core], i, partner)
    wait(gram.at[1 - core], i, partner)
    for copy in sent:
        copy.wait_send()


def gram_kernel(dims, left, gram_out, left_out, both, part, z_in, y_in, gram, send, recv):
    place = Place(*dims)
    greet([place.partner()] + place.x_peers() + place.y_peers() + place.z_peers())
    gram_steps(place, left, both, part, z_in, y_in, gram, send, recv)
    half = left.shape[1]
    rows = left.shape[0] // 2
    own = pl.ds(pl.multiple_of(place.core * rows, 8), rows)
    for c in range(2):
        gram_out[:, c * half : (c + 1) * half] = gram[c]
        left_out[:, c * half : (c + 1) * half] = both[c, own, :]


def gram_call(dims, left):
    nz, ny, nx = dims
    rows, half = left.shape
    rank = 2 * half
    across = rank // nx
    sems = 2 + 2 * nz + ny + nx
    return pl.pallas_call(
        functools.partial(gram_kernel, dims),
        out_shape=(
            jax.ShapeDtypeStruct((rank, rank), F32),
            jax.ShapeDtypeStruct((rows // 2, rank), F32),
        ),
        in_specs=[VMEM_SPEC],
        out_specs=(VMEM_SPEC,) * 2,
        scratch_shapes=[
            pltpu.VMEM((2, rows, half), F32),
            pltpu.VMEM((across, half), F32),
            pltpu.VMEM((nz, across // nz, half), F32),
            pltpu.VMEM((ny, across // nz, half), F32),
            pltpu.VMEM((2, rank, half), F32),
            pltpu.SemaphoreType.DMA((sems,)),
            pltpu.SemaphoreType.DMA((sems,)),
        ],
        compiler_params=pltpu.CompilerParams(
            collective_id=1, has_side_effects=True, vmem_limit_bytes=VMEM_LIMIT
        ),
        name="gram",
    )(left)


def factor_kernel(gram, left, w, ortho, a):
    a[...] = gram[...]
    run_all(factor_steps(a, w))
    ortho[...] = exact_dot(left[...], w[...], 1, 1)


def factor_call(gram, left):
    rank = gram.shape[0]
    return pl.pallas_call(
        factor_kernel,
        out_shape=(
            jax.ShapeDtypeStruct((rank, rank), F32),
            jax.ShapeDtypeStruct(left.shape, F32),
        ),
        in_specs=[VMEM_SPEC] * 2,
        out_specs=(VMEM_SPEC,) * 2,
        scratch_shapes=[pltpu.VMEM((rank, rank), F32)],
        compiler_params=pltpu.CompilerParams(vmem_limit_bytes=VMEM_LIMIT),
        name="factor",
    )(gram, left)


def project(pair, left, total):
    columns = pair.shape[2]
    half = left.shape[1]
    upper = left[...].astype(BF16)
    lower = (left[...] - upper.astype(F32)).astype(BF16)
    both = jnp.concatenate([upper, lower], axis=1)
    rows = pair.shape[1]
    width = 512 if columns % 512 == 0 else BLOCK

    @pl.loop(0, columns // width)
    def _(i):
        at = pl.ds(pl.multiple_of(i * width, BLOCK), width)
        value = sum(
            lax.dot_general(pair[c, :, at], both[c * rows : (c + 1) * rows], (((0,), (0,)), ((), ())),
                            preferred_element_type=F32)
            for c in range(2)
        )
        total[at, :] = value[:, :half] + value[:, half:]


def right_kernel(dims, pair, left, w, right, right_half, squares, total, inbox_a, inbox_b, both,
                 ring_send, ring_recv, swap_send, swap_recv):
    place = Place(*dims)
    core, partner = place.core, place.partner()
    half = left.shape[1]
    piece = both.shape[1]
    shard = piece // 2
    greet([partner] + place.neighbours())
    project(pair, left, total)

    def scatter(geometry):
        run_all(reduce_plane(total, inbox_a, inbox_b, piece, ssem=ring_send, rsem=ring_recv, **geometry))

    pl.when(core == 0)(lambda: scatter(row_first(place)))
    pl.when(core == 1)(lambda: scatter(column_first(place)))
    own = pl.ds(pl.multiple_of(place.chip() * piece, 8), piece)
    swap = remote(total.at[own, :], both.at[core], swap_send, swap_recv, partner)
    swap.start()
    both[core] = total[own, :]
    swap.wait_recv()
    value = exact_dot(both[0], w[:, :half], 1, 1) + exact_dot(both[1], w[:, half:], 1, 1)
    right[...] = jnp.where(core == 0, value[:shard], value[shard:])
    right_half[...] = jnp.where(core == 0, value[:, :half], value[:, half:]).astype(BF16)
    squares[...] = jnp.broadcast_to(jnp.sum(value * value, axis=0, keepdims=True), squares.shape)
    swap.wait_send()


def right_call(dims, pair, left, w):
    nz, ny, nx = dims
    columns = pair.shape[2]
    half = left.shape[1]
    rank = 2 * half
    chips = nz * ny
    piece = columns // chips
    ring = chips + max(nz, ny)
    dma = pltpu.SemaphoreType.DMA
    return pl.pallas_call(
        functools.partial(right_kernel, dims),
        out_shape=(
            jax.ShapeDtypeStruct((piece // 2, rank), F32),
            jax.ShapeDtypeStruct((piece, half), BF16),
            jax.ShapeDtypeStruct((8, rank), F32),
        ),
        in_specs=[VMEM_SPEC] * 3,
        out_specs=(VMEM_SPEC,) * 3,
        scratch_shapes=[
            pltpu.VMEM((columns, half), F32),
            pltpu.VMEM((chips, piece, half), F32),
            pltpu.VMEM((max(nz, ny), piece, half), F32),
            pltpu.VMEM((2, piece, half), F32),
            dma((ring,)), dma((ring,)), dma, dma,
        ],
        compiler_params=pltpu.CompilerParams(
            collective_id=2, has_side_effects=True, vmem_limit_bytes=VMEM_LIMIT
        ),
        name="right_factor",
    )(pair, left, w)


def share_kernel(dims, right_half, squares, gathered, norms, z_in, y_in, x_in,
                 ring_send, ring_recv, swap_send, swap_recv, send, recv):
    place = Place(*dims)
    nz, ny, nx = dims
    core, partner = place.core, place.partner()
    piece = right_half.shape[0]
    greet([partner] + place.x_peers() + place.y_peers() + place.z_peers())
    buf = gathered.at[core]
    at = lambda slot: pl.ds(pl.multiple_of(slot * piece, 16), piece)
    buf[at(place.chip()), :] = right_half[...]

    def level(inbox, me, peers, count, base, value):
        inbox[me] = value
        for o, peer in enumerate(peers, 1):
            remote(inbox.at[me], inbox.at[me], send.at[base + o], recv.at[base + o], peer).start()

    def level_done(inbox, me, peers, count, base):
        for o, peer in enumerate(peers, 1):
            there = inbox.at[wrap(me - o, count)]
            remote(there, there, send.at[base + o], recv.at[base + o], peer).wait_recv()
        total = inbox[0]
        for i in range(1, count):
            total = total + inbox[i]
        return total

    def drain(inbox, me, peers, base):
        for o, peer in enumerate(peers, 1):
            remote(inbox.at[me], inbox.at[me], send.at[base + o], recv.at[base + o], peer).wait_send()

    z_level = (z_in, place.z, place.z_peers(), nz, 0)
    y_level = (y_in, place.y, place.y_peers(), ny, nz)
    x_level = (x_in, place.x, place.x_peers(), nx, nz + ny)

    level(*z_level, squares[...])

    def after_z():
        level(*y_level, level_done(*z_level))

    def after_y():
        level(*x_level, level_done(*y_level))

    def after_x():
        norms[...] = level_done(*x_level)

    def forward(slot):
        here = buf.at[at(slot), :]
        remote(here, here, swap_send.at[slot], swap_recv.at[slot], partner).start()

    def run(geometry):
        gather_plane(buf, piece, ssem=ring_send, rsem=ring_recv, done=forward,
                     extras=(after_z, after_y, after_x), **geometry)

    pl.when(core == 0)(lambda: run(column_first(place)))
    pl.when(core == 1)(lambda: run(row_first(place)))

    for slot in range(nz * ny):
        there = gathered.at[1 - core, slot * piece : (slot + 1) * piece, :]
        remote(there, there, swap_send.at[slot], swap_recv.at[slot], partner).wait_recv()
    for slot in range(nz * ny):
        here = gathered.at[core, slot * piece : (slot + 1) * piece, :]
        remote(here, here, swap_send.at[slot], swap_recv.at[slot], partner).wait_send()
    for inbox, me, peers, count, base in (z_level, y_level, x_level):
        drain(inbox, me, peers, base)


def share_call(dims, right_half, squares):
    nz, ny, nx = dims
    piece, half = right_half.shape
    chips = nz * ny
    ring = chips + max(nz, ny)
    rank = 2 * half
    dma = pltpu.SemaphoreType.DMA
    return pl.pallas_call(
        functools.partial(share_kernel, dims),
        out_shape=(
            jax.ShapeDtypeStruct((2, chips * piece, half), BF16),
            jax.ShapeDtypeStruct((8, rank), F32),
        ),
        in_specs=[VMEM_SPEC] * 2,
        out_specs=(VMEM_SPEC,) * 2,
        scratch_shapes=[
            pltpu.VMEM((nz, 8, rank), F32),
            pltpu.VMEM((ny, 8, rank), F32),
            pltpu.VMEM((nx, 8, rank), F32),
            dma((ring,)), dma((ring,)), dma((chips,)), dma((chips,)),
            dma((nz + ny + nx,)), dma((nz + ny + nx,)),
        ],
        compiler_params=pltpu.CompilerParams(
            collective_id=3, has_side_effects=True, vmem_limit_bytes=VMEM_LIMIT
        ),
        name="share_right",
    )(right_half, squares)


def apply_kernel(step, momentum, gradient, ortho_half, update_left, gathered, momentum_next, update):
    half = gathered.shape[2]
    dims = (((1,), (1,)), ((), ()))

    def product(left):
        return sum(
            lax.dot_general(left[:, c * half : (c + 1) * half], gathered[c], dims, preferred_element_type=F32)
            for c in range(2)
        )

    blended = momentum[...] + gradient[...].astype(F32)
    momentum_next[...] = blended - step * product(ortho_half[...])
    update[...] = product(update_left[...]).astype(BF16)


def apply_call(step, momentum, gradient, ortho_half, update_left, gathered):
    rows, columns = momentum.shape
    rank = ortho_half.shape[1]
    width = 512 if columns % 512 == 0 else BLOCK
    tile = pl.BlockSpec((rows, width), lambda i: (0, i))
    whole = pl.BlockSpec((rows, rank), lambda i: (0, 0))
    return pl.pallas_call(
        functools.partial(apply_kernel, step),
        grid=(columns // width,),
        out_shape=(
            jax.ShapeDtypeStruct((rows, columns), F32),
            jax.ShapeDtypeStruct((rows, columns), BF16),
        ),
        in_specs=[tile, tile, whole, whole, pl.BlockSpec((2, width, rank // 2), lambda i: (0, i, 0))],
        out_specs=(tile, tile),
        compiler_params=pltpu.CompilerParams(vmem_limit_bytes=VMEM_LIMIT),
        name="apply",
    )(momentum, gradient, ortho_half, update_left, gathered)


def local(dims, momentum, gradient, right_prior):
    decay = 0.95
    prior = right_prior[0]
    blend_half = (momentum + gradient.astype(F32)).astype(BF16)
    left, pair = left_factor_call(dims, blend_half, prior)
    gram, left_rows = gram_call(dims, left)
    w, orthonormal = factor_call(gram, left_rows)
    right, right_half, squares = right_call(dims, pair, left, w)
    gathered, norms = share_call(dims, right_half, squares)
    column_scale = 1.0 / jnp.sqrt(norms[:1] + 1e-06)
    right_next = (right * column_scale).astype(BF16)[None]
    rows_all = momentum.shape[0] * lax.axis_size("fsdp")
    cols_all = momentum.shape[1] * lax.axis_size("tp")
    magnitude = math.sqrt(rows_all * cols_all / prior.shape[1])
    ortho_half = orthonormal.astype(BF16)
    update_left = (orthonormal * column_scale * magnitude).astype(BF16)
    momentum_next, update = apply_call(1.0 - decay, momentum, gradient, ortho_half, update_left, gathered)
    return (momentum_next, update, right_next)


def solution(mesh):
    fsdp, tp = mesh.shape["fsdp"], mesh.shape["tp"]
    dims = (fsdp // (2 * Y_CHIPS), Y_CHIPS, tp)
    in_specs = (P("fsdp", "tp"), P("fsdp", "tp"), P("tp", "fsdp", None))
    out_specs = (P("fsdp", "tp"), P("fsdp", "tp"), P("tp", "fsdp", None))
    return jax.shard_map(
        functools.partial(local, dims), mesh=mesh, in_specs=in_specs, out_specs=out_specs, check_vma=False
    )
```

```python
import functools
import math

import jax
import jax.numpy as jnp
from jax import lax
from jax.experimental import pallas as pl
from jax.experimental.pallas import tpu as pltpu
from jax.sharding import PartitionSpec as P

HIGHEST = lax.Precision.HIGHEST
MESH = pl.DeviceIdType.MESH
F32 = jnp.float32
BF16 = jnp.bfloat16
VMEM_SPEC = pl.BlockSpec(memory_space=pltpu.VMEM)
VMEM_LIMIT = 60 * 1024 * 1024
BLOCK = 128
Y_CHIPS = 4


def wrap(value, size):
    return lax.rem(value + size, size)


def exact_dot(a, b, a_dim, b_dim):
    return lax.dot_general(
        a, b, (((a_dim,), (b_dim,)), ((), ())), precision=HIGHEST, preferred_element_type=F32
    )


class Place:
    def __init__(self, nz, ny, nx):
        self.nz, self.ny, self.nx = nz, ny, nx
        index = lax.axis_index("fsdp")
        self.x = lax.axis_index("tp")
        self.core = lax.rem(index, 2)
        self.y = lax.rem(lax.div(index, 2), ny)
        self.z = lax.div(index, 2 * ny)

    def device(self, z=None, y=None, core=None, x=None):
        z = self.z if z is None else z
        y = self.y if y is None else y
        core = self.core if core is None else core
        x = self.x if x is None else x
        return ((z * self.ny + y) * 2 + core, x)

    def partner(self):
        return self.device(core=1 - self.core)

    def x_peers(self):
        return [self.device(x=wrap(self.x + o, self.nx)) for o in range(1, self.nx)]

    def y_peers(self):
        return [self.device(y=wrap(self.y + o, self.ny)) for o in range(1, self.ny)]

    def z_peers(self):
        return [self.device(z=wrap(self.z + o, self.nz)) for o in range(1, self.nz)]

    def chip(self):
        return self.z * self.ny + self.y


def greet(devices):
    barrier = pltpu.get_barrier_semaphore()
    for device in devices:
        pl.semaphore_signal(barrier, inc=1, device_id=device, device_id_type=MESH)
    pl.semaphore_wait(barrier, len(devices))


def remote(src, dst, send_sem, recv_sem, device):
    return pltpu.make_async_remote_copy(
        src_ref=src, dst_ref=dst, send_sem=send_sem, recv_sem=recv_sem,
        device_id=device, device_id_type=MESH,
    )


def halves(rows, unit):
    first = -(-(rows // 2) // unit) * unit
    return ((0, first), (first, rows - first))


class Plan:
    def __init__(self, place, z_first, offset, rows, unit):
        self.offset, self.rows = offset, rows
        first = -(-(rows // 2) // unit) * unit
        self.spans = ((0, first), (first, rows - first))
        self.unit = unit
        if z_first:
            self.na, self.nb, self.me_a, self.me_b = place.nz, place.ny, place.z, place.y
            self.slot = lambda a, b: a * place.ny + b
            self.device = lambda a, b: place.device(z=a, y=b)
        else:
            self.na, self.nb, self.me_a, self.me_b = place.ny, place.nz, place.y, place.z
            self.slot = lambda a, b: b * place.ny + a
            self.device = lambda a, b: place.device(z=b, y=a)
        self.half_a, self.half_b = self.na // 2, self.nb // 2
        self.sems = self.na + self.na * self.nb

    def span(self, part):
        return (0, self.rows) if part is None else self.spans[part]

    def at(self, a, b, piece, part=None):
        offset, size = self.span(part)
        start = self.slot(a, b) * piece + self.offset + offset
        return pl.ds(pl.multiple_of(start, self.unit), size)


def gather_events(plan, buf, piece, ssem, rsem, base, done):
    na, nb, half_a, half_b = plan.na, plan.nb, plan.half_a, plan.half_b
    me_a, me_b = plan.me_a, plan.me_b

    def copy(key, sending):
        kind, d, step, ra = key
        sign = 1 - 2 * d
        if kind == 0:
            part = d if step == half_a else None
            back = (0 if step <= 2 else 2) if sending else step
            a, b = wrap(me_a - sign * back, na), me_b
            target = plan.device(wrap(me_a + sign * (step - back), na), me_b)
            index = base + d * half_a + step - 1
        else:
            part = d if step == half_b else None
            a, b = wrap(me_a + ra, na), wrap(me_b - sign * (step - 1 if sending else step), nb)
            target = plan.device(me_a, wrap(me_b + sign, nb))
            index = base + na + (d * half_b + step - 1) * na + ra
        ref = buf.at[plan.at(a, b, piece, part), :]
        return remote(ref, ref, ssem.at[index], rsem.at[index], target)

    started = []

    def start(key):
        copy(key, True).start()
        started.append(key)

    def spread(ra):
        for d in (0, 1):
            start((1, d, 1, ra))

    landed = {}

    def whole(what):
        landed[what] = landed.get(what, 0) + 1
        return landed[what] == 2

    def begin():
        for step in range(1, min(half_a, 2) + 1):
            for d in (0, 1):
                start((0, d, step, 0))
        spread(0)
        done(plan, me_a, me_b)

    def first_ring(d, step):
        sign = 1 - 2 * d
        copy((0, d, step, 0), False).wait_recv()
        if step == 2:
            for later in range(3, half_a + 1):
                start((0, d, later, 0))
        if step < half_a or whole("a"):
            ra = (-sign * step) % na
            spread(ra)
            done(plan, wrap(me_a + ra, na), me_b)

    def second_ring(d, step, ra):
        sign = 1 - 2 * d
        copy((1, d, step, ra), False).wait_recv()
        if step < half_b:
            start((1, d, step + 1, ra))
        if step < half_b or whole(ra):
            done(plan, wrap(me_a + ra, na), wrap(me_b - sign * step, nb))

    def end():
        for key in started:
            copy(key, True).wait_send()

    when = {0: 0.0, 1: 1.0, 2: 1.4, 3: 2.4, 4: 2.8}
    events = []
    for step in range(1, half_a + 1):
        for d in (0, 1):
            events.append((when[step], functools.partial(first_ring, d, step)))
    for step in range(1, half_b + 1):
        for ra in range(na):
            for d in (0, 1):
                events.append((when[min(ra, na - ra)] + 0.05 + step, functools.partial(second_ring, d, step, ra)))
    return begin, events, end


def gather_plane(buf, piece, plans, ssem, rsem, done, extras=()):
    base, events, begins, ends = 0, [], [], []
    for plan in plans:
        begin, some, end = gather_events(plan, buf, piece, ssem, rsem, base, done)
        base += plan.sems
        begins.append(begin)
        ends.append(end)
        events += some
    for begin in begins:
        begin()
    events += list(extras)
    for _, action in sorted(events, key=lambda e: e[0]):
        action()
    for end in ends:
        end()


def far_first(n):
    return sorted(range(n), key=lambda j: (-min(j, n - j), j))


def reduce_events(plan, total, inbox_a, inbox_b, piece, ssem, rsem, base, per_chunk, hop):
    order = far_first(plan.nb)

    def ring(n, me, chunks, source, inbox, device, base):
        half = n // 2

        def index(d, step, j):
            return base + (d * half + step - 1) * len(chunks) + chunks.index(j)

        def landing(d, step, j, part):
            offset, size = plan.span(part)
            slot = (d * half + step - 1) * len(chunks) + chunks.index(j)
            return inbox.at[slot, pl.ds(offset, size), :]

        def copy(d, step, j):
            sign = 1 - 2 * d
            part = d if step == 1 else None
            if step == 1:
                src = total.at[source(wrap(me - sign * half, n), j, part), :]
            else:
                src = landing(d, step - 1, j, part)
            i = index(d, step, j)
            return remote(src, landing(d, step, j, part), ssem.at[i], rsem.at[i], device(wrap(me - sign, n)))

        def send(j):
            for d in (0, 1):
                copy(d, 1, j).start()

        def receive(d, step, j):
            sign = 1 - 2 * d
            copy(d, step, j).wait_recv()
            if step < half:
                dest = wrap(me - sign * (half - step), n)
                for part in (0, 1):
                    here = landing(d, step, j, part)
                    own = total[source(dest, j, part), :]
                    here[...] = own if step == 1 and part != d else here[...] + own
                copy(d, step + 1, j).start()
            else:
                part = d if step == 1 else None
                own = source(me, j, part)
                total[own, :] = total[own, :] + landing(d, step, j, part)[...]

        def end():
            for step in range(1, half + 1):
                for j in chunks:
                    for d in (0, 1):
                        copy(d, step, j).wait_send()

        return send, receive, end

    na, nb = plan.na, plan.nb
    send_a, receive_a, end_a = ring(
        na, plan.me_a, order,
        lambda dest, j, part: plan.at(dest, wrap(plan.me_b + j, nb), piece, part),
        inbox_a, lambda a: plan.device(a, plan.me_b), base,
    )
    send_b, receive_b, end_b = ring(
        nb, plan.me_b, [0],
        lambda dest, j, part: plan.at(plan.me_a, dest, piece, part),
        inbox_b, lambda b: plan.device(plan.me_a, b), base + na * nb,
    )
    events = []
    ready = {}
    for pos, j in enumerate(order):
        events.append((max(0.0, per_chunk * (pos - 1)), functools.partial(send_a, j)))
        for step in range(1, plan.half_a + 1):
            at = per_chunk * pos + hop * step
            for d in (0, 1):
                events.append((at + 0.01 * d, functools.partial(receive_a, d, step, j)))
        ready[min(j, nb - j)] = per_chunk * pos + hop * plan.half_a + 0.1
    events.append((ready[plan.half_b], functools.partial(send_b, 0)))
    at = ready[plan.half_b]
    for step in range(1, plan.half_b + 1):
        at = max(at + hop, ready[plan.half_b - step] + 0.1)
        for d in (0, 1):
            events.append((at + 0.01 * d, functools.partial(receive_b, d, step, 0)))

    def end():
        end_a()
        end_b()

    return events, end


def rows_of(tile, k):
    return jnp.broadcast_to(tile[k : k + 1, :], tile.shape)


def columns_of(tile, k):
    return jnp.broadcast_to(tile[:, k : k + 1], tile.shape)


def inverse_factor(block):
    count = BLOCK // 8
    d = [block[8 * i : 8 * i + 8, :] for i in range(count)]
    row = lax.broadcasted_iota(jnp.int32, (8, BLOCK), 0)
    lane = lax.broadcasted_iota(jnp.int32, (8, BLOCK), 1)
    e = [(row + 8 * i == lane).astype(F32) for i in range(count)]
    out = []
    for s in range(count):
        c = [[columns_of(d[i], 8 * s + k) for k in range(8)] for i in range(s, count)]
        pivots = jnp.zeros((8, BLOCK), F32)
        for k in range(8):
            pivot = rows_of(c[0][k], k)
            inverse = 1.0 / pivot
            pivots = jnp.where(row == k, pivot, pivots)
            d_row, e_row = rows_of(d[s], k), rows_of(e[s], k)
            later = [rows_of(c[0][q], k) for q in range(k + 1, 8)]
            for i in range(s, count):
                factor = c[i - s][k] * inverse
                if i == s:
                    factor = jnp.where(row > k, factor, 0.0)
                d[i] = d[i] - factor * d_row
                e[i] = e[i] - factor * e_row
                for q in range(k + 1, 8):
                    c[i - s][q] = c[i - s][q] - factor * later[q - k - 1]
        out.append(e[s] * lax.rsqrt(pivots))
        if s % 2:
            yield 0.6
    return jnp.concatenate(out, axis=0)


def factor_steps(a, w):
    size = a.shape[0]
    w[...] = jnp.zeros((size, size), F32)
    for o in range(0, size, BLOCK):
        end = o + BLOCK
        inverse = yield from inverse_factor(a[o:end, o:end])
        w[o:end, o:end] = inverse
        if end < size:
            low = exact_dot(a[end:, o:end], inverse, 1, 1)
            a[end:, o:end] = low
            a[end:, end:] = a[end:, end:] - exact_dot(low, low, 1, 1)
        yield 0.5
        if o:
            through = exact_dot(a[o:end, :o], w[:o, :o], 1, 0)
            w[o:end, :o] = -exact_dot(inverse, through, 1, 0)
        yield 0.3


class Mail:
    def __init__(self, send, recv):
        self.send, self.recv, self.used, self.sent = send, recv, 0, []

    def take(self, count):
        self.used += count
        return self.used - count

    def start(self, src, dst, index, device):
        copy = remote(src, dst, self.send.at[index], self.recv.at[index], device)
        copy.start()
        self.sent.append(copy)

    def wait(self, ref, index, device):
        remote(ref, ref, self.send.at[index], self.recv.at[index], device).wait_recv()

    def end(self):
        for copy in self.sent:
            copy.wait_send()


def left_sum(place, mail, partial, inbox, left):
    nx = place.nx
    part = partial.shape[0] // nx
    peers = place.x_peers()
    at = lambda x: pl.ds(pl.multiple_of(x * part, 8), part)
    base = mail.take(nx)
    for o, peer in enumerate(peers, 1):
        mail.start(partial.at[at(wrap(place.x + o, nx)), :], inbox.at[o], base + o, peer)
    total = partial[at(place.x), :]
    for o, peer in enumerate(peers, 1):
        mail.wait(inbox.at[o], base + o, peer)
        total = total + inbox[o]
    left[at(place.x), :] = total
    base = mail.take(nx)
    for o, peer in enumerate(peers, 1):
        mail.start(left.at[at(place.x), :], left.at[at(place.x), :], base + o, peer)
    for o, peer in enumerate(peers, 1):
        mail.wait(left.at[at(wrap(place.x - o, nx)), :], base + o, peer)


def gram_steps(place, mail, left, both, part, z_in, y_in, gram, meanwhile):
    core, partner = place.core, place.partner()
    nz, ny, nx = place.nz, place.ny, place.nx
    half = left.shape[1]
    across = 2 * half // nx
    rows = across // nz

    i = mail.take(1)
    mail.start(left, both.at[core], i, partner)
    both[core] = left[...]
    mail.wait(both.at[1 - core], i, partner)
    per = half // across
    lanes = pl.ds(pl.multiple_of(lax.rem(place.x, per) * across, BLOCK), across)
    part[...] = exact_dot(both[lax.div(place.x, per), :, lanes], left[...], 0, 0)

    z_peers, y_peers, x_peers = place.z_peers(), place.y_peers(), place.x_peers()
    at_z = lambda z: pl.ds(pl.multiple_of(z * rows, 8), rows)
    i = mail.take(nz)
    for o, peer in enumerate(z_peers, 1):
        mail.start(part.at[at_z(wrap(place.z + o, nz)), :], z_in.at[o], i + o, peer)
    meanwhile()
    yield 0.0
    total = part[at_z(place.z), :]
    for o, peer in enumerate(z_peers, 1):
        mail.wait(z_in.at[o], i + o, peer)
        total = total + z_in[o]
    i = mail.take(ny)
    y_in[place.y] = total
    for o, peer in enumerate(y_peers, 1):
        mail.start(y_in.at[place.y], y_in.at[place.y], i + o, peer)
    yield 3.5
    for o, peer in enumerate(y_peers, 1):
        mail.wait(y_in.at[wrap(place.y - o, ny)], i + o, peer)
    total = y_in[0]
    for y in range(1, ny):
        total = total + y_in[y]

    def at(x, z):
        return gram.at[core, pl.ds(pl.multiple_of(x * across + z * rows, 8), rows), :]

    at(place.x, place.z)[...] = total
    i = mail.take(nz)
    for o, peer in enumerate(z_peers, 1):
        mail.start(at(place.x, place.z), at(place.x, place.z), i + o, peer)
    yield 5.0
    for o, peer in enumerate(z_peers, 1):
        mail.wait(at(place.x, wrap(place.z - o, nz)), i + o, peer)
    whole = lambda x: gram.at[core, pl.ds(pl.multiple_of(x * across, 8), across), :]
    i = mail.take(nx)
    for o, peer in enumerate(x_peers, 1):
        mail.start(whole(place.x), whole(place.x), i + o, peer)
    yield 5.5
    for o, peer in enumerate(x_peers, 1):
        mail.wait(whole(wrap(place.x - o, nx)), i + o, peer)
    i = mail.take(1)
    mail.start(gram.at[core], gram.at[core], i, partner)
    yield 1.5
    mail.wait(gram.at[1 - core], i, partner)


def project(pair, left, total):
    rows, columns = pair.shape[1:]
    half = left.shape[1]
    upper = left[...].astype(BF16)
    lower = (left[...] - upper.astype(F32)).astype(BF16)
    both = jnp.concatenate([upper, lower], axis=1)
    width = 512 if columns % 512 == 0 else BLOCK

    @pl.loop(0, columns // width)
    def _(i):
        at = pl.ds(pl.multiple_of(i * width, BLOCK), width)
        value = sum(
            lax.dot_general(pair[c, :, at], both[c * rows : (c + 1) * rows], (((0,), (0,)), ((), ())),
                            preferred_element_type=F32)
            for c in range(2)
        )
        total[at, :] = value[:, :half] + value[:, half:]


def merge(steps, events, begin=0.0):
    events = sorted(events, key=lambda e: e[0])
    now = begin
    for spent in steps:
        now += spent
        while events and events[0][0] <= now:
            events.pop(0)[1]()
    for _, action in events:
        action()


def step_kernel(dims, magnitude, momentum, gradient, prior, gathered, stacked, right_next,
                mom, grad, pair, mine, given, buf, partial, x_in, left, both, part, z_in, y_in, gram,
                a, w, total, in_yz, in_z, in_zy, in_y, pieces, ortho, nz_in, ny_in, nx_in,
                load_sem, one_send, one_recv, two_send, two_recv, sum_send, sum_recv,
                swap_send, swap_recv, send, recv):
    place = Place(*dims)
    nz, ny, nx = dims
    core, partner = place.core, place.partner()
    shard, rank = prior.shape
    half = rank // 2
    rows, columns = mom.shape
    piece = 2 * shard
    long = 128 if piece == 208 else 32
    loads = [pltpu.make_async_copy(momentum, mom, load_sem.at[0]), pltpu.make_async_copy(gradient, grad, load_sem.at[1])]
    for load in loads:
        load.start()
    greet([partner] + place.x_peers() + place.y_peers() + place.z_peers())
    mail = Mail(send, recv)

    low, high = prior[:, :half].astype(F32), prior[:, half:].astype(F32)
    given[...] = jnp.where(core == 0, high, low)
    at_mine = mine.at[pl.ds(pl.multiple_of(core * shard, 8), shard), :]
    at_theirs = mine.at[pl.ds(pl.multiple_of((1 - core) * shard, 8), shard), :]
    i = mail.take(1)
    mail.start(given, at_mine, i, partner)
    at_mine[...] = jnp.where(core == 0, low, high)
    mail.wait(at_theirs, i, partner)
    at_chip = lambda slot: pl.ds(pl.multiple_of(slot * piece, 16), piece)
    buf[at_chip(place.chip()), :] = mine[...].astype(BF16)
    swap_blend = mail.take(1)

    def blend():
        for load in loads:
            load.wait()
        width = 512 if columns % 512 == 0 else BLOCK

        @pl.loop(0, columns // width)
        def _(i):
            at = pl.ds(pl.multiple_of(i * width, BLOCK), width)
            pair[core, :, at] = (mom[:, at] + grad[:, at].astype(F32)).astype(BF16)

        mail.start(pair.at[core], pair.at[core], swap_blend, partner)

    plans = lambda unit: (Plan(place, True, 0, long, unit), Plan(place, False, long, piece - long, unit))
    gather_plane(buf, piece, plans(16), one_send, one_recv, lambda *_: None, [(0.5, blend)])
    mail.wait(pair.at[1 - core], swap_blend, partner)

    width = 1664 if columns % 1664 == 0 else BLOCK
    partial[...] = jnp.zeros_like(partial)

    @pl.loop(0, columns // width)
    def _(i):
        at = pl.ds(pl.multiple_of(i * width, BLOCK), width)
        for c in range(2):
            own = slice(c * rows, (c + 1) * rows)
            partial[own, :] += jnp.dot(pair[c, :, at], buf[at, :], preferred_element_type=F32)

    left_sum(place, mail, partial, x_in, left)

    bulk_y = Plan(place, False, 0, long, 8)
    bulk_z = Plan(place, True, long, piece - long, 8)
    events_y, end_y = reduce_events(bulk_y, total, in_yz, in_z, piece, sum_send, sum_recv, 0, 4.5, 4.5)
    events_z, end_z = reduce_events(bulk_z, total, in_zy, in_y, piece, sum_send, sum_recv, nz * ny + nz, 6.6, 4.0)

    def chain():
        yield from gram_steps(place, mail, left, both, part, z_in, y_in, gram, lambda: project(pair, left, total))
        for c in range(2):
            a[:, c * half : (c + 1) * half] = gram[c]
        yield from factor_steps(a, w)
        own = pl.ds(pl.multiple_of(core * rows, 8), rows)
        ortho[...] = exact_dot(both[0, own, :], w[:, :half], 1, 1) + exact_dot(both[1, own, :], w[:, half:], 1, 1)
        yield 1.0

    merge(chain(), events_y + events_z)

    own = pl.ds(pl.multiple_of(place.chip() * piece, 8), piece)
    i = mail.take(1)
    mail.start(total.at[own, :], pieces.at[core], i, partner)
    pieces[core] = total[own, :]
    mail.wait(pieces.at[1 - core], i, partner)
    value = exact_dot(pieces[0], w[:, :half], 1, 1) + exact_dot(pieces[1], w[:, half:], 1, 1)
    squares = jnp.broadcast_to(jnp.sum(value * value, axis=0, keepdims=True), (8, rank))
    right = jnp.where(core == 0, value[:shard], value[shard:])
    share = gathered.at[core]
    share[at_chip(place.chip()), :] = jnp.where(core == 0, value[:, :half], value[:, half:]).astype(BF16)

    def level(inbox, me, peers, count):
        return inbox, me, peers, count, mail.take(count)

    def level_start(inbox, me, peers, count, base, value):
        inbox[me] = value
        for o, peer in enumerate(peers, 1):
            mail.start(inbox.at[me], inbox.at[me], base + o, peer)

    def level_done(inbox, me, peers, count, base):
        for o, peer in enumerate(peers, 1):
            mail.wait(inbox.at[wrap(me - o, count)], base + o, peer)
        total = inbox[0]
        for i in range(1, count):
            total = total + inbox[i]
        return total

    z_level = level(nz_in, place.z, place.z_peers(), nz)
    y_level = level(ny_in, place.y, place.y_peers(), ny)
    x_level = level(nx_in, place.x, place.x_peers(), nx)
    level_start(*z_level, squares)

    def finish():
        column_scale = 1.0 / jnp.sqrt(level_done(*x_level)[:1] + 1e-06)
        right_next[...] = (right * column_scale).astype(BF16)
        stacked[:rows, :] = ortho[...].astype(BF16)
        stacked[rows:, :] = (ortho[...] * column_scale * magnitude).astype(BF16)

    def forward(plan, a, b):
        offset = 0 if plan.offset == 0 else nz * ny
        here = share.at[plan.at(a, b, piece), :]
        slot = offset + plan.slot(a, b)
        remote(here, here, swap_send.at[slot], swap_recv.at[slot], partner).start()

    gather_plane(share, piece, plans(16), two_send, two_recv, forward, [
        (1.2, lambda: level_start(*y_level, level_done(*z_level))),
        (2.0, lambda: level_start(*x_level, level_done(*y_level))),
        (3.0, finish),
    ])
    for offset, size, base in ((0, long, 0), (long, piece - long, nz * ny)):
        for slot in range(nz * ny):
            at = slice(slot * piece + offset, slot * piece + offset + size)
            there, here = gathered.at[1 - core, at, :], gathered.at[core, at, :]
            remote(there, there, swap_send.at[base + slot], swap_recv.at[base + slot], partner).wait_recv()
            remote(here, here, swap_send.at[base + slot], swap_recv.at[base + slot], partner).wait_send()
    end_y()
    end_z()
    mail.end()


def step_call(dims, magnitude, momentum, gradient, prior):
    nz, ny, nx = dims
    shard, rank = prior.shape
    rows, columns = momentum.shape
    half = rank // 2
    piece = 2 * shard
    long = 128 if piece == 208 else 32
    chips = nz * ny
    across = rank // nx
    ring = 2 * chips + nz + ny
    mails = 5 + 4 * nx + 3 * nz + 2 * ny
    dma = pltpu.SemaphoreType.DMA
    vmem = pltpu.VMEM
    return pl.pallas_call(
        functools.partial(step_kernel, dims, magnitude),
        out_shape=(
            jax.ShapeDtypeStruct((2, columns, half), BF16),
            jax.ShapeDtypeStruct((2 * rows, rank), BF16),
            jax.ShapeDtypeStruct((shard, rank), BF16),
        ),
        in_specs=[pl.BlockSpec(memory_space=pl.ANY)] * 2 + [VMEM_SPEC],
        out_specs=(VMEM_SPEC,) * 3,
        scratch_shapes=[
            vmem((rows, columns), F32), vmem((rows, columns), BF16),
            vmem((2, rows, columns), BF16),
            vmem((piece, half), F32), vmem((shard, half), F32), vmem((columns, half), BF16),
            vmem((2 * rows, half), F32), vmem((nx, 2 * rows // nx, half), F32), vmem((2 * rows, half), F32),
            vmem((2, 2 * rows, half), F32), vmem((across, half), F32),
            vmem((nz, across // nz, half), F32), vmem((ny, across // nz, half), F32),
            vmem((2, rank, half), F32), vmem((rank, rank), F32), vmem((rank, rank), F32),
            vmem((columns, half), F32),
            vmem((chips, long, half), F32), vmem((nz, long, half), F32),
            vmem((chips, piece - long, half), F32), vmem((ny, piece - long, half), F32),
            vmem((2, piece, half), F32), vmem((rows, rank), F32),
            vmem((nz, 8, rank), F32), vmem((ny, 8, rank), F32), vmem((nx, 8, rank), F32),
            dma((2,)), dma((ring,)), dma((ring,)), dma((ring,)), dma((ring,)), dma((ring,)), dma((ring,)),
            dma((2 * chips,)), dma((2 * chips,)), dma((mails,)), dma((mails,)),
        ],
        compiler_params=pltpu.CompilerParams(
            collective_id=0, has_side_effects=True, vmem_limit_bytes=VMEM_LIMIT
        ),
        name="dion_step",
    )(momentum, gradient, prior)


def apply_kernel(step, momentum, gradient, stacked, gathered, momentum_next, update):
    half = gathered.shape[2]
    rows = momentum.shape[0]
    dims = (((1,), (1,)), ((), ()))
    products = sum(
        lax.dot_general(stacked[:, c * half : (c + 1) * half], gathered[c], dims, preferred_element_type=F32)
        for c in range(2)
    )
    blended = momentum[...] + gradient[...].astype(F32)
    momentum_next[...] = blended - step * products[:rows]
    update[...] = products[rows:].astype(BF16)


def apply_call(step, momentum, gradient, stacked, gathered):
    rows, columns = momentum.shape
    rank = stacked.shape[1]
    width = 512 if columns % 512 == 0 else BLOCK
    tile = pl.BlockSpec((rows, width), lambda i: (0, i))
    return pl.pallas_call(
        functools.partial(apply_kernel, step),
        grid=(columns // width,),
        out_shape=(
            jax.ShapeDtypeStruct((rows, columns), F32),
            jax.ShapeDtypeStruct((rows, columns), BF16),
        ),
        in_specs=[
            tile, tile, pl.BlockSpec(stacked.shape, lambda i: (0, 0)),
            pl.BlockSpec((2, width, rank // 2), lambda i: (0, i, 0)),
        ],
        out_specs=(tile, tile),
        compiler_params=pltpu.CompilerParams(vmem_limit_bytes=VMEM_LIMIT),
        name="apply",
    )(momentum, gradient, stacked, gathered)


def local(dims, momentum, gradient, right_prior):
    decay = 0.95
    prior = right_prior[0]
    rows_all = momentum.shape[0] * lax.axis_size("fsdp")
    cols_all = momentum.shape[1] * lax.axis_size("tp")
    magnitude = math.sqrt(rows_all * cols_all / prior.shape[1])
    gathered, stacked, right_next = step_call(dims, magnitude, momentum, gradient, prior)
    momentum_next, update = apply_call(1.0 - decay, momentum, gradient, stacked, gathered)
    return (momentum_next, update, right_next[None])


def solution(mesh):
    fsdp, tp = mesh.shape["fsdp"], mesh.shape["tp"]
    dims = (fsdp // (2 * Y_CHIPS), Y_CHIPS, tp)
    in_specs = (P("fsdp", "tp"), P("fsdp", "tp"), P("tp", "fsdp", None))
    out_specs = (P("fsdp", "tp"), P("fsdp", "tp"), P("tp", "fsdp", None))
    return jax.shard_map(
        functools.partial(local, dims), mesh=mesh, in_specs=in_specs, out_specs=out_specs, check_vma=False
    )
```

```python
import functools
import math

import jax
import jax.numpy as jnp
from jax import lax
from jax.experimental import pallas as pl
from jax.experimental.pallas import tpu as pltpu
from jax.sharding import PartitionSpec as P

PER_Y, HOP_Y, PER_Z, HOP_Z = 4.5, 4.5, 9.0, 4.0
GRAM_TIMES = (0.0, 3.5, 5.0, 5.5, 1.5)
FACTOR_SCALE = 1.0
SUM_LONG = 128
WHEN = {0: 0.0, 1: 1.0, 2: 1.4, 3: 2.4, 4: 2.8}
PACE_Y, PACE_Z = 1.0, 1.0

HIGHEST = lax.Precision.HIGHEST
MESH = pl.DeviceIdType.MESH
F32 = jnp.float32
BF16 = jnp.bfloat16
VMEM_SPEC = pl.BlockSpec(memory_space=pltpu.VMEM)
VMEM_LIMIT = 60 * 1024 * 1024
BLOCK = 128
Y_CHIPS = 4


def wrap(value, size):
    return lax.rem(value + size, size)


def exact_dot(a, b, a_dim, b_dim):
    return lax.dot_general(
        a, b, (((a_dim,), (b_dim,)), ((), ())), precision=HIGHEST, preferred_element_type=F32
    )


class Place:
    def __init__(self, nz, ny, nx):
        self.nz, self.ny, self.nx = nz, ny, nx
        index = lax.axis_index("fsdp")
        self.x = lax.axis_index("tp")
        self.core = lax.rem(index, 2)
        self.y = lax.rem(lax.div(index, 2), ny)
        self.z = lax.div(index, 2 * ny)

    def device(self, z=None, y=None, core=None, x=None):
        z = self.z if z is None else z
        y = self.y if y is None else y
        core = self.core if core is None else core
        x = self.x if x is None else x
        return ((z * self.ny + y) * 2 + core, x)

    def partner(self):
        return self.device(core=1 - self.core)

    def x_peers(self):
        return [self.device(x=wrap(self.x + o, self.nx)) for o in range(1, self.nx)]

    def y_peers(self):
        return [self.device(y=wrap(self.y + o, self.ny)) for o in range(1, self.ny)]

    def z_peers(self):
        return [self.device(z=wrap(self.z + o, self.nz)) for o in range(1, self.nz)]

    def chip(self):
        return self.z * self.ny + self.y


def greet(devices):
    barrier = pltpu.get_barrier_semaphore()
    for device in devices:
        pl.semaphore_signal(barrier, inc=1, device_id=device, device_id_type=MESH)
    pl.semaphore_wait(barrier, len(devices))


def remote(src, dst, send_sem, recv_sem, device):
    return pltpu.make_async_remote_copy(
        src_ref=src, dst_ref=dst, send_sem=send_sem, recv_sem=recv_sem,
        device_id=device, device_id_type=MESH,
    )


def halves(rows, unit):
    first = -(-(rows // 2) // unit) * unit
    return ((0, first), (first, rows - first))


class Plan:
    def __init__(self, place, z_first, offset, rows, unit):
        self.offset, self.rows = offset, rows
        first = -(-(rows // 2) // unit) * unit
        self.spans = ((0, first), (first, rows - first))
        self.unit = unit
        if z_first:
            self.na, self.nb, self.me_a, self.me_b = place.nz, place.ny, place.z, place.y
            self.slot = lambda a, b: a * place.ny + b
            self.device = lambda a, b: place.device(z=a, y=b)
        else:
            self.na, self.nb, self.me_a, self.me_b = place.ny, place.nz, place.y, place.z
            self.slot = lambda a, b: b * place.ny + a
            self.device = lambda a, b: place.device(z=b, y=a)
        self.half_a, self.half_b = self.na // 2, self.nb // 2
        self.sems = self.na + self.na * self.nb

    def span(self, part):
        return (0, self.rows) if part is None else self.spans[part]

    def at(self, a, b, piece, part=None):
        offset, size = self.span(part)
        start = self.slot(a, b) * piece + self.offset + offset
        return pl.ds(pl.multiple_of(start, self.unit), size)


def gather_events(plan, buf, piece, ssem, rsem, base, done):
    na, nb, half_a, half_b = plan.na, plan.nb, plan.half_a, plan.half_b
    me_a, me_b = plan.me_a, plan.me_b

    def copy(key, sending):
        kind, d, step, ra = key
        sign = 1 - 2 * d
        if kind == 0:
            part = d if step == half_a else None
            back = (0 if step <= 2 else 2) if sending else step
            a, b = wrap(me_a - sign * back, na), me_b
            target = plan.device(wrap(me_a + sign * (step - back), na), me_b)
            index = base + d * half_a + step - 1
        else:
            part = d if step == half_b else None
            a, b = wrap(me_a + ra, na), wrap(me_b - sign * (step - 1 if sending else step), nb)
            target = plan.device(me_a, wrap(me_b + sign, nb))
            index = base + na + (d * half_b + step - 1) * na + ra
        ref = buf.at[plan.at(a, b, piece, part), :]
        return remote(ref, ref, ssem.at[index], rsem.at[index], target)

    started = []

    def start(key):
        copy(key, True).start()
        started.append(key)

    def spread(ra):
        for d in (0, 1):
            start((1, d, 1, ra))

    landed = {}

    def whole(what):
        landed[what] = landed.get(what, 0) + 1
        return landed[what] == 2

    def begin():
        for step in range(1, min(half_a, 2) + 1):
            for d in (0, 1):
                start((0, d, step, 0))
        spread(0)
        done(plan, me_a, me_b)

    def first_ring(d, step):
        sign = 1 - 2 * d
        copy((0, d, step, 0), False).wait_recv()
        if step == 2:
            for later in range(3, half_a + 1):
                start((0, d, later, 0))
        if step < half_a or whole("a"):
            ra = (-sign * step) % na
            spread(ra)
            done(plan, wrap(me_a + ra, na), me_b)

    def second_ring(d, step, ra):
        sign = 1 - 2 * d
        copy((1, d, step, ra), False).wait_recv()
        if step < half_b:
            start((1, d, step + 1, ra))
        if step < half_b or whole(ra):
            done(plan, wrap(me_a + ra, na), wrap(me_b - sign * step, nb))

    def end():
        for key in started:
            copy(key, True).wait_send()

    when, pace = WHEN, PACE_Y if plan.half_b == 2 else PACE_Z
    events = []
    for step in range(1, half_a + 1):
        for d in (0, 1):
            events.append((when[step], functools.partial(first_ring, d, step)))
    for step in range(1, half_b + 1):
        for ra in range(na):
            for d in (0, 1):
                events.append((when[min(ra, na - ra)] + 0.05 + pace * step, functools.partial(second_ring, d, step, ra)))
    return begin, events, end


def gather_plane(buf, piece, plans, ssem, rsem, done, extras=()):
    base, events, begins, ends = 0, [], [], []
    for plan in plans:
        begin, some, end = gather_events(plan, buf, piece, ssem, rsem, base, done)
        base += plan.sems
        begins.append(begin)
        ends.append(end)
        events += some
    for begin in begins:
        begin()
    events += list(extras)
    for _, action in sorted(events, key=lambda e: e[0]):
        action()
    for end in ends:
        end()


def far_first(n):
    return sorted(range(n), key=lambda j: (-min(j, n - j), j))


def reduce_events(plan, total, inbox_a, inbox_b, piece, ssem, rsem, base, per_chunk, hop):
    order = far_first(plan.nb)

    def ring(n, me, chunks, source, inbox, device, base):
        half = n // 2

        def index(d, step, j):
            return base + (d * half + step - 1) * len(chunks) + chunks.index(j)

        def landing(d, step, j, part):
            offset, size = plan.span(part)
            slot = (d * half + step - 1) * len(chunks) + chunks.index(j)
            return inbox.at[slot, pl.ds(offset, size), :]

        def copy(d, step, j):
            sign = 1 - 2 * d
            part = d if step == 1 else None
            if step == 1:
                src = total.at[source(wrap(me - sign * half, n), j, part), :]
            else:
                src = landing(d, step - 1, j, part)
            i = index(d, step, j)
            return remote(src, landing(d, step, j, part), ssem.at[i], rsem.at[i], device(wrap(me - sign, n)))

        def send(j):
            for d in (0, 1):
                copy(d, 1, j).start()

        def receive(d, step, j):
            sign = 1 - 2 * d
            copy(d, step, j).wait_recv()
            if step < half:
                dest = wrap(me - sign * (half - step), n)
                for part in (0, 1):
                    here = landing(d, step, j, part)
                    own = total[source(dest, j, part), :]
                    here[...] = own if step == 1 and part != d else here[...] + own
                copy(d, step + 1, j).start()
            else:
                part = d if step == 1 else None
                own = source(me, j, part)
                total[own, :] = total[own, :] + landing(d, step, j, part)[...]

        def end():
            for step in range(1, half + 1):
                for j in chunks:
                    for d in (0, 1):
                        copy(d, step, j).wait_send()

        return send, receive, end

    na, nb = plan.na, plan.nb
    send_a, receive_a, end_a = ring(
        na, plan.me_a, order,
        lambda dest, j, part: plan.at(dest, wrap(plan.me_b + j, nb), piece, part),
        inbox_a, lambda a: plan.device(a, plan.me_b), base,
    )
    send_b, receive_b, end_b = ring(
        nb, plan.me_b, [0],
        lambda dest, j, part: plan.at(plan.me_a, dest, piece, part),
        inbox_b, lambda b: plan.device(plan.me_a, b), base + na * nb,
    )
    events = []
    ready = {}
    for pos, j in enumerate(order):
        events.append((0.0 if pos == 0 else max(0.1, per_chunk * (pos - 1)), functools.partial(send_a, j)))
        for step in range(1, plan.half_a + 1):
            at = per_chunk * pos + hop * step
            for d in (0, 1):
                events.append((at + 0.01 * d, functools.partial(receive_a, d, step, j)))
        ready[min(j, nb - j)] = per_chunk * pos + hop * plan.half_a + 0.1
    events.append((ready[plan.half_b], functools.partial(send_b, 0)))
    at = ready[plan.half_b]
    for step in range(1, plan.half_b + 1):
        at = max(at + hop, ready[plan.half_b - step] + 0.1)
        for d in (0, 1):
            events.append((at + 0.01 * d, functools.partial(receive_b, d, step, 0)))

    def end():
        end_a()
        end_b()

    return events, end


def rows_of(tile, k):
    return jnp.broadcast_to(tile[k : k + 1, :], tile.shape)


def columns_of(tile, k):
    return jnp.broadcast_to(tile[:, k : k + 1], tile.shape)


def inverse_factor(block):
    count = BLOCK // 8
    d = [block[8 * i : 8 * i + 8, :] for i in range(count)]
    row = lax.broadcasted_iota(jnp.int32, (8, BLOCK), 0)
    lane = lax.broadcasted_iota(jnp.int32, (8, BLOCK), 1)
    e = [(row + 8 * i == lane).astype(F32) for i in range(count)]
    out = []
    for s in range(count):
        c = [[columns_of(d[i], 8 * s + k) for k in range(8)] for i in range(s, count)]
        pivots = jnp.zeros((8, BLOCK), F32)
        for k in range(8):
            pivot = rows_of(c[0][k], k)
            inverse = 1.0 / pivot
            pivots = jnp.where(row == k, pivot, pivots)
            d_row, e_row = rows_of(d[s], k), rows_of(e[s], k)
            later = [rows_of(c[0][q], k) for q in range(k + 1, 8)]
            for i in range(s, count):
                factor = c[i - s][k] * inverse
                if i == s:
                    factor = jnp.where(row > k, factor, 0.0)
                d[i] = d[i] - factor * d_row
                e[i] = e[i] - factor * e_row
                for q in range(k + 1, 8):
                    c[i - s][q] = c[i - s][q] - factor * later[q - k - 1]
        out.append(e[s] * lax.rsqrt(pivots))
        if s % 2:
            yield 0.072 * (17 - s) * FACTOR_SCALE
    return jnp.concatenate(out, axis=0)


def factor_steps(a, w):
    size = a.shape[0]
    w[...] = jnp.zeros((size, size), F32)
    for o in range(0, size, BLOCK):
        end = o + BLOCK
        inverse = yield from inverse_factor(a[o:end, o:end])
        w[o:end, o:end] = inverse
        if end < size:
            low = exact_dot(a[end:, o:end], inverse, 1, 1)
            a[end:, o:end] = low
            a[end:, end:] = a[end:, end:] - exact_dot(low, low, 1, 1)
        yield 0.5 * FACTOR_SCALE
        if o:
            through = exact_dot(a[o:end, :o], w[:o, :o], 1, 0)
            w[o:end, :o] = -exact_dot(inverse, through, 1, 0)
        yield 0.3 * FACTOR_SCALE


class Mail:
    def __init__(self, send, recv):
        self.send, self.recv, self.used, self.sent = send, recv, 0, []

    def take(self, count):
        self.used += count
        return self.used - count

    def start(self, src, dst, index, device):
        copy = remote(src, dst, self.send.at[index], self.recv.at[index], device)
        copy.start()
        self.sent.append(copy)

    def wait(self, ref, index, device):
        remote(ref, ref, self.send.at[index], self.recv.at[index], device).wait_recv()

    def end(self):
        for copy in self.sent:
            copy.wait_send()


def left_sum(place, mail, partial, inbox, left):
    nx = place.nx
    part = partial.shape[0] // nx
    peers = place.x_peers()
    at = lambda x: pl.ds(pl.multiple_of(x * part, 8), part)
    base = mail.take(nx)
    for o, peer in enumerate(peers, 1):
        mail.start(partial.at[at(wrap(place.x + o, nx)), :], inbox.at[o], base + o, peer)
    total = partial[at(place.x), :]
    for o, peer in enumerate(peers, 1):
        mail.wait(inbox.at[o], base + o, peer)
        total = total + inbox[o]
    left[at(place.x), :] = total
    base = mail.take(nx)
    for o, peer in enumerate(peers, 1):
        mail.start(left.at[at(place.x), :], left.at[at(place.x), :], base + o, peer)
    for o, peer in enumerate(peers, 1):
        mail.wait(left.at[at(wrap(place.x - o, nx)), :], base + o, peer)


def gram_steps(place, mail, left, both, part, z_in, y_in, gram, meanwhile):
    core, partner = place.core, place.partner()
    nz, ny, nx = place.nz, place.ny, place.nx
    half = left.shape[1]
    across = 2 * half // nx
    rows = across // nz

    i = mail.take(1)
    mail.start(left, both.at[core], i, partner)
    both[core] = left[...]
    mail.wait(both.at[1 - core], i, partner)
    per = half // across
    lanes = pl.ds(pl.multiple_of(lax.rem(place.x, per) * across, BLOCK), across)
    part[...] = exact_dot(both[lax.div(place.x, per), :, lanes], left[...], 0, 0)

    z_peers, y_peers, x_peers = place.z_peers(), place.y_peers(), place.x_peers()
    at_z = lambda z: pl.ds(pl.multiple_of(z * rows, 8), rows)
    i = mail.take(nz)
    for o, peer in enumerate(z_peers, 1):
        mail.start(part.at[at_z(wrap(place.z + o, nz)), :], z_in.at[o], i + o, peer)
    meanwhile()
    yield GRAM_TIMES[0]
    total = part[at_z(place.z), :]
    for o, peer in enumerate(z_peers, 1):
        mail.wait(z_in.at[o], i + o, peer)
        total = total + z_in[o]
    i = mail.take(ny)
    y_in[place.y] = total
    for o, peer in enumerate(y_peers, 1):
        mail.start(y_in.at[place.y], y_in.at[place.y], i + o, peer)
    yield GRAM_TIMES[1]
    for o, peer in enumerate(y_peers, 1):
        mail.wait(y_in.at[wrap(place.y - o, ny)], i + o, peer)
    total = y_in[0]
    for y in range(1, ny):
        total = total + y_in[y]

    def at(x, z):
        return gram.at[core, pl.ds(pl.multiple_of(x * across + z * rows, 8), rows), :]

    at(place.x, place.z)[...] = total
    i = mail.take(nz)
    for o, peer in enumerate(z_peers, 1):
        mail.start(at(place.x, place.z), at(place.x, place.z), i + o, peer)
    yield GRAM_TIMES[2]
    for o, peer in enumerate(z_peers, 1):
        mail.wait(at(place.x, wrap(place.z - o, nz)), i + o, peer)
    whole = lambda x: gram.at[core, pl.ds(pl.multiple_of(x * across, 8), across), :]
    i = mail.take(nx)
    for o, peer in enumerate(x_peers, 1):
        mail.start(whole(place.x), whole(place.x), i + o, peer)
    yield GRAM_TIMES[3]
    for o, peer in enumerate(x_peers, 1):
        mail.wait(whole(wrap(place.x - o, nx)), i + o, peer)
    i = mail.take(1)
    mail.start(gram.at[core], gram.at[core], i, partner)
    yield GRAM_TIMES[4]
    mail.wait(gram.at[1 - core], i, partner)


def split_terms(left):
    upper = left[...].astype(BF16)
    lower = (left[...] - upper.astype(F32)).astype(BF16)
    return jnp.concatenate([upper, lower], axis=1)


def project(pair, terms, total, begin, size):
    rows = pair.shape[1]
    half = total.shape[1]
    width = next(w for w in (832, 512, 384, BLOCK) if size % w == 0 and w % BLOCK == 0)

    @pl.loop(0, size // width)
    def _(i):
        at = pl.ds(pl.multiple_of(begin + i * width, BLOCK), width)
        value = sum(
            lax.dot_general(pair[c, :, at], terms[c * rows : (c + 1) * rows, :], (((0,), (0,)), ((), ())),
                            preferred_element_type=F32)
            for c in range(2)
        )
        total[at, :] = value[:, :half] + value[:, half:]


def merge(steps, events, begin=0.0):
    events = sorted(events, key=lambda e: e[0])
    now = begin
    for spent in steps:
        now += spent
        while events and events[0][0] <= now:
            events.pop(0)[1]()
    for _, action in events:
        action()


def step_kernel(dims, magnitude, momentum, gradient, prior, gathered, stacked, right_next,
                mom, grad, pair, mine, given, buf, partial, x_in, left, both, part, z_in, y_in, gram,
                a, w, total, terms, in_yz, in_z, in_zy, in_y, pieces, ortho, nz_in, ny_in, nx_in,
                load_sem, one_send, one_recv, two_send, two_recv, sum_send, sum_recv,
                swap_send, swap_recv, send, recv):
    place = Place(*dims)
    nz, ny, nx = dims
    core, partner = place.core, place.partner()
    shard, rank = prior.shape
    half = rank // 2
    rows, columns = mom.shape
    piece = 2 * shard
    long = 128 if piece == 208 else 32
    loads = [pltpu.make_async_copy(momentum, mom, load_sem.at[0]), pltpu.make_async_copy(gradient, grad, load_sem.at[1])]
    for load in loads:
        load.start()
    greet([partner] + place.x_peers() + place.y_peers() + place.z_peers())
    mail = Mail(send, recv)

    low, high = prior[:, :half].astype(F32), prior[:, half:].astype(F32)
    given[...] = jnp.where(core == 0, high, low)
    at_mine = mine.at[pl.ds(pl.multiple_of(core * shard, 8), shard), :]
    at_theirs = mine.at[pl.ds(pl.multiple_of((1 - core) * shard, 8), shard), :]
    i = mail.take(1)
    mail.start(given, at_mine, i, partner)
    at_mine[...] = jnp.where(core == 0, low, high)
    mail.wait(at_theirs, i, partner)
    at_chip = lambda slot: pl.ds(pl.multiple_of(slot * piece, 16), piece)
    buf[at_chip(place.chip()), :] = mine[...].astype(BF16)
    swap_blend = mail.take(1)

    def blend():
        for load in loads:
            load.wait()
        width = 512 if columns % 512 == 0 else BLOCK

        @pl.loop(0, columns // width)
        def _(i):
            at = pl.ds(pl.multiple_of(i * width, BLOCK), width)
            pair[core, :, at] = (mom[:, at] + grad[:, at].astype(F32)).astype(BF16)

        mail.start(pair.at[core], pair.at[core], swap_blend, partner)

    plans = lambda unit: (Plan(place, True, 0, long, unit), Plan(place, False, long, piece - long, unit))
    gather_plane(buf, piece, plans(16), one_send, one_recv, lambda *_: None, [(0.5, blend)])
    mail.wait(pair.at[1 - core], swap_blend, partner)

    width = 1664 if columns % 1664 == 0 else BLOCK
    partial[...] = jnp.zeros_like(partial)

    @pl.loop(0, columns // width)
    def _(i):
        at = pl.ds(pl.multiple_of(i * width, BLOCK), width)
        for c in range(2):
            own = slice(c * rows, (c + 1) * rows)
            partial[own, :] += jnp.dot(pair[c, :, at], buf[at, :], preferred_element_type=F32)

    left_sum(place, mail, partial, x_in, left)

    sum_long = SUM_LONG if piece == 208 else 32
    bulk_y = Plan(place, False, 0, sum_long, 8)
    bulk_z = Plan(place, True, sum_long, piece - sum_long, 8)
    events_y, end_y = reduce_events(bulk_y, total, in_yz, in_z, piece, sum_send, sum_recv, 0, PER_Y, HOP_Y)
    events_z, end_z = reduce_events(bulk_z, total, in_zy, in_y, piece, sum_send, sum_recv, nz * ny + nz, PER_Z, HOP_Z)

    terms[...] = split_terms(left)
    parts = nz // 2
    size = columns // parts

    def project_part(ahead):
        start = wrap(lax.div(place.z, 2) + ahead, parts) * size
        project(pair, terms, total, start, size)

    first = parts // 2
    others = sorted((k for k in range(parts) if k != first), key=lambda k: (-min(k, parts - k), k))
    events_part = [(0.05, functools.partial(project_part, k)) for k in others]

    def chain():
        yield from gram_steps(place, mail, left, both, part, z_in, y_in, gram, lambda: project_part(first))
        for c in range(2):
            a[:, c * half : (c + 1) * half] = gram[c]
        yield from factor_steps(a, w)
        own = pl.ds(pl.multiple_of(core * rows, 8), rows)
        ortho[...] = exact_dot(both[0, own, :], w[:, :half], 1, 1) + exact_dot(both[1, own, :], w[:, half:], 1, 1)
        yield 1.0

    merge(chain(), events_y + events_z + events_part)

    own = pl.ds(pl.multiple_of(place.chip() * piece, 8), piece)
    i = mail.take(1)
    mail.start(total.at[own, :], pieces.at[core], i, partner)
    pieces[core] = total[own, :]
    mail.wait(pieces.at[1 - core], i, partner)
    value = exact_dot(pieces[0], w[:, :half], 1, 1) + exact_dot(pieces[1], w[:, half:], 1, 1)
    squares = jnp.broadcast_to(jnp.sum(value * value, axis=0, keepdims=True), (8, rank))
    right = jnp.where(core == 0, value[:shard], value[shard:])
    share = gathered.at[core]
    share[at_chip(place.chip()), :] = jnp.where(core == 0, value[:, :half], value[:, half:]).astype(BF16)

    def level(inbox, me, peers, count):
        return inbox, me, peers, count, mail.take(count)

    def level_start(inbox, me, peers, count, base, value):
        inbox[me] = value
        for o, peer in enumerate(peers, 1):
            mail.start(inbox.at[me], inbox.at[me], base + o, peer)

    def level_done(inbox, me, peers, count, base):
        for o, peer in enumerate(peers, 1):
            mail.wait(inbox.at[wrap(me - o, count)], base + o, peer)
        total = inbox[0]
        for i in range(1, count):
            total = total + inbox[i]
        return total

    z_level = level(nz_in, place.z, place.z_peers(), nz)
    y_level = level(ny_in, place.y, place.y_peers(), ny)
    x_level = level(nx_in, place.x, place.x_peers(), nx)
    level_start(*z_level, squares)

    def finish():
        column_scale = 1.0 / jnp.sqrt(level_done(*x_level)[:1] + 1e-06)
        right_next[...] = (right * column_scale).astype(BF16)
        stacked[:rows, :] = ortho[...].astype(BF16)
        stacked[rows:, :] = (ortho[...] * column_scale * magnitude).astype(BF16)

    def forward(plan, a, b):
        offset = 0 if plan.offset == 0 else nz * ny
        here = share.at[plan.at(a, b, piece), :]
        slot = offset + plan.slot(a, b)
        remote(here, here, swap_send.at[slot], swap_recv.at[slot], partner).start()

    gather_plane(share, piece, plans(16), two_send, two_recv, forward, [
        (1.2, lambda: level_start(*y_level, level_done(*z_level))),
        (2.0, lambda: level_start(*x_level, level_done(*y_level))),
        (3.0, finish),
    ])
    for offset, size, base in ((0, long, 0), (long, piece - long, nz * ny)):
        for slot in range(nz * ny):
            at = slice(slot * piece + offset, slot * piece + offset + size)
            there, here = gathered.at[1 - core, at, :], gathered.at[core, at, :]
            remote(there, there, swap_send.at[base + slot], swap_recv.at[base + slot], partner).wait_recv()
            remote(here, here, swap_send.at[base + slot], swap_recv.at[base + slot], partner).wait_send()
    end_y()
    end_z()
    mail.end()


def step_call(dims, magnitude, momentum, gradient, prior):
    nz, ny, nx = dims
    shard, rank = prior.shape
    rows, columns = momentum.shape
    half = rank // 2
    piece = 2 * shard
    long = 128 if piece == 208 else 32
    sum_long = SUM_LONG if piece == 208 else 32
    chips = nz * ny
    across = rank // nx
    ring = 2 * chips + nz + ny
    mails = 5 + 4 * nx + 3 * nz + 2 * ny
    dma = pltpu.SemaphoreType.DMA
    vmem = pltpu.VMEM
    return pl.pallas_call(
        functools.partial(step_kernel, dims, magnitude),
        out_shape=(
            jax.ShapeDtypeStruct((2, columns, half), BF16),
            jax.ShapeDtypeStruct((2 * rows, rank), BF16),
            jax.ShapeDtypeStruct((shard, rank), BF16),
        ),
        in_specs=[pl.BlockSpec(memory_space=pl.ANY)] * 2 + [VMEM_SPEC],
        out_specs=(VMEM_SPEC,) * 3,
        scratch_shapes=[
            vmem((rows, columns), F32), vmem((rows, columns), BF16),
            vmem((2, rows, columns), BF16),
            vmem((piece, half), F32), vmem((shard, half), F32), vmem((columns, half), BF16),
            vmem((2 * rows, half), F32), vmem((nx, 2 * rows // nx, half), F32), vmem((2 * rows, half), F32),
            vmem((2, 2 * rows, half), F32), vmem((across, half), F32),
            vmem((nz, across // nz, half), F32), vmem((ny, across // nz, half), F32),
            vmem((2, rank, half), F32), vmem((rank, rank), F32), vmem((rank, rank), F32),
            vmem((columns, half), F32), vmem((2 * rows, rank), BF16),
            vmem((chips, sum_long, half), F32), vmem((nz, sum_long, half), F32),
            vmem((chips, piece - sum_long, half), F32), vmem((ny, piece - sum_long, half), F32),
            vmem((2, piece, half), F32), vmem((rows, rank), F32),
            vmem((nz, 8, rank), F32), vmem((ny, 8, rank), F32), vmem((nx, 8, rank), F32),
            dma((2,)), dma((ring,)), dma((ring,)), dma((ring,)), dma((ring,)), dma((ring,)), dma((ring,)),
            dma((2 * chips,)), dma((2 * chips,)), dma((mails,)), dma((mails,)),
        ],
        compiler_params=pltpu.CompilerParams(
            collective_id=0, has_side_effects=True, vmem_limit_bytes=VMEM_LIMIT
        ),
        name="dion_step",
    )(momentum, gradient, prior)


def apply_kernel(step, momentum, gradient, stacked, gathered, momentum_next, update):
    half = gathered.shape[2]
    rows = momentum.shape[0]
    dims = (((1,), (1,)), ((), ()))
    products = sum(
        lax.dot_general(stacked[:, c * half : (c + 1) * half], gathered[c], dims, preferred_element_type=F32)
        for c in range(2)
    )
    blended = momentum[...] + gradient[...].astype(F32)
    momentum_next[...] = blended - step * products[:rows]
    update[...] = products[rows:].astype(BF16)


def apply_call(step, momentum, gradient, stacked, gathered):
    rows, columns = momentum.shape
    rank = stacked.shape[1]
    width = columns // 2 if columns % 256 == 0 else BLOCK
    tile = pl.BlockSpec((rows, width), lambda i: (0, i))
    return pl.pallas_call(
        functools.partial(apply_kernel, step),
        grid=(columns // width,),
        out_shape=(
            jax.ShapeDtypeStruct((rows, columns), F32),
            jax.ShapeDtypeStruct((rows, columns), BF16),
        ),
        in_specs=[
            tile, tile, pl.BlockSpec(stacked.shape, lambda i: (0, 0)),
            pl.BlockSpec((2, width, rank // 2), lambda i: (0, i, 0)),
        ],
        out_specs=(tile, tile),
        compiler_params=pltpu.CompilerParams(vmem_limit_bytes=VMEM_LIMIT),
        name="apply",
    )(momentum, gradient, stacked, gathered)


def local(dims, momentum, gradient, right_prior):
    decay = 0.95
    prior = right_prior[0]
    rows_all = momentum.shape[0] * lax.axis_size("fsdp")
    cols_all = momentum.shape[1] * lax.axis_size("tp")
    magnitude = math.sqrt(rows_all * cols_all / prior.shape[1])
    gathered, stacked, right_next = step_call(dims, magnitude, momentum, gradient, prior)
    momentum_next, update = apply_call(1.0 - decay, momentum, gradient, stacked, gathered)
    return (momentum_next, update, right_next[None])


def solution(mesh):
    fsdp, tp = mesh.shape["fsdp"], mesh.shape["tp"]
    dims = (fsdp // (2 * Y_CHIPS), Y_CHIPS, tp)
    in_specs = (P("fsdp", "tp"), P("fsdp", "tp"), P("tp", "fsdp", None))
    out_specs = (P("fsdp", "tp"), P("fsdp", "tp"), P("tp", "fsdp", None))
    return jax.shard_map(
        functools.partial(local, dims), mesh=mesh, in_specs=in_specs, out_specs=out_specs, check_vma=False
    )
```

```python
import functools
import math

import jax
import jax.numpy as jnp
from jax import lax
from jax.experimental import pallas as pl
from jax.experimental.pallas import tpu as pltpu
from jax.sharding import PartitionSpec as P

PER_Y, HOP_Y, PER_Z, HOP_Z = 4.5, 4.5, 9.0, 4.0
GRAM_TIMES = (1.0, 4.5, 6.0, 7.5, 3.0)
FACTOR_SCALE = 1.0
SUM_LONG = 128
WHEN = {0: 0.0, 1: 1.0, 2: 1.4, 3: 2.4, 4: 2.8}
PACE_Y, PACE_Z = 1.0, 1.0

HIGHEST = lax.Precision.HIGHEST
MESH = pl.DeviceIdType.MESH
F32 = jnp.float32
BF16 = jnp.bfloat16
VMEM_SPEC = pl.BlockSpec(memory_space=pltpu.VMEM)
VMEM_LIMIT = 60 * 1024 * 1024
BLOCK = 128
Y_CHIPS = 4


def wrap(value, size):
    return lax.rem(value + size, size)


def exact_dot(a, b, a_dim, b_dim):
    return lax.dot_general(
        a, b, (((a_dim,), (b_dim,)), ((), ())), precision=HIGHEST, preferred_element_type=F32
    )


class Place:
    def __init__(self, nz, ny, nx):
        self.nz, self.ny, self.nx = nz, ny, nx
        index = lax.axis_index("fsdp")
        self.x = lax.axis_index("tp")
        self.core = lax.rem(index, 2)
        self.y = lax.rem(lax.div(index, 2), ny)
        self.z = lax.div(index, 2 * ny)

    def device(self, z=None, y=None, core=None, x=None):
        z = self.z if z is None else z
        y = self.y if y is None else y
        core = self.core if core is None else core
        x = self.x if x is None else x
        return ((z * self.ny + y) * 2 + core, x)

    def partner(self):
        return self.device(core=1 - self.core)

    def x_peers(self):
        return [self.device(x=wrap(self.x + o, self.nx)) for o in range(1, self.nx)]

    def y_peers(self):
        return [self.device(y=wrap(self.y + o, self.ny)) for o in range(1, self.ny)]

    def z_peers(self):
        return [self.device(z=wrap(self.z + o, self.nz)) for o in range(1, self.nz)]

    def chip(self):
        return self.z * self.ny + self.y


def greet(devices):
    barrier = pltpu.get_barrier_semaphore()
    for device in devices:
        pl.semaphore_signal(barrier, inc=1, device_id=device, device_id_type=MESH)
    pl.semaphore_wait(barrier, len(devices))


def remote(src, dst, send_sem, recv_sem, device):
    return pltpu.make_async_remote_copy(
        src_ref=src, dst_ref=dst, send_sem=send_sem, recv_sem=recv_sem,
        device_id=device, device_id_type=MESH,
    )


def halves(rows, unit):
    first = -(-(rows // 2) // unit) * unit
    return ((0, first), (first, rows - first))


class Plan:
    def __init__(self, place, z_first, offset, rows, unit):
        self.offset, self.rows = offset, rows
        first = -(-(rows // 2) // unit) * unit
        self.spans = ((0, first), (first, rows - first))
        self.unit = unit
        if z_first:
            self.na, self.nb, self.me_a, self.me_b = place.nz, place.ny, place.z, place.y
            self.slot = lambda a, b: a * place.ny + b
            self.device = lambda a, b: place.device(z=a, y=b)
        else:
            self.na, self.nb, self.me_a, self.me_b = place.ny, place.nz, place.y, place.z
            self.slot = lambda a, b: b * place.ny + a
            self.device = lambda a, b: place.device(z=b, y=a)
        self.half_a, self.half_b = self.na // 2, self.nb // 2
        self.sems = self.na + self.na * self.nb

    def span(self, part):
        return (0, self.rows) if part is None else self.spans[part]

    def at(self, a, b, piece, part=None):
        offset, size = self.span(part)
        start = self.slot(a, b) * piece + self.offset + offset
        return pl.ds(pl.multiple_of(start, self.unit), size)


def gather_events(plan, buf, piece, ssem, rsem, base, done):
    na, nb, half_a, half_b = plan.na, plan.nb, plan.half_a, plan.half_b
    me_a, me_b = plan.me_a, plan.me_b

    def copy(key, sending):
        kind, d, step, ra = key
        sign = 1 - 2 * d
        if kind == 0:
            part = d if step == half_a else None
            back = (0 if step <= 2 else 2) if sending else step
            a, b = wrap(me_a - sign * back, na), me_b
            target = plan.device(wrap(me_a + sign * (step - back), na), me_b)
            index = base + d * half_a + step - 1
        else:
            part = d if step == half_b else None
            a, b = wrap(me_a + ra, na), wrap(me_b - sign * (step - 1 if sending else step), nb)
            target = plan.device(me_a, wrap(me_b + sign, nb))
            index = base + na + (d * half_b + step - 1) * na + ra
        ref = buf.at[plan.at(a, b, piece, part), :]
        return remote(ref, ref, ssem.at[index], rsem.at[index], target)

    started = []

    def start(key):
        copy(key, True).start()
        started.append(key)

    def spread(ra):
        for d in (0, 1):
            start((1, d, 1, ra))

    landed = {}

    def whole(what):
        landed[what] = landed.get(what, 0) + 1
        return landed[what] == 2

    def begin():
        for step in range(1, min(half_a, 2) + 1):
            for d in (0, 1):
                start((0, d, step, 0))
        spread(0)
        done(plan, me_a, me_b)

    def first_ring(d, step):
        sign = 1 - 2 * d
        copy((0, d, step, 0), False).wait_recv()
        if step == 2:
            for later in range(3, half_a + 1):
                start((0, d, later, 0))
        if step < half_a or whole("a"):
            ra = (-sign * step) % na
            spread(ra)
            done(plan, wrap(me_a + ra, na), me_b)

    def second_ring(d, step, ra):
        sign = 1 - 2 * d
        copy((1, d, step, ra), False).wait_recv()
        if step < half_b:
            start((1, d, step + 1, ra))
        if step < half_b or whole(ra):
            done(plan, wrap(me_a + ra, na), wrap(me_b - sign * step, nb))

    def end():
        for key in started:
            copy(key, True).wait_send()

    when, pace = WHEN, PACE_Y if plan.half_b == 2 else PACE_Z
    events = []
    for step in range(1, half_a + 1):
        for d in (0, 1):
            events.append((when[step], functools.partial(first_ring, d, step)))
    for step in range(1, half_b + 1):
        for ra in range(na):
            for d in (0, 1):
                events.append((when[min(ra, na - ra)] + 0.05 + pace * step, functools.partial(second_ring, d, step, ra)))
    return begin, events, end


def gather_plane(buf, piece, plans, ssem, rsem, done, extras=()):
    base, events, begins, ends = 0, [], [], []
    for plan in plans:
        begin, some, end = gather_events(plan, buf, piece, ssem, rsem, base, done)
        base += plan.sems
        begins.append(begin)
        ends.append(end)
        events += some
    for begin in begins:
        begin()
    events += list(extras)
    for _, action in sorted(events, key=lambda e: e[0]):
        action()
    for end in ends:
        end()


def far_first(n):
    return sorted(range(n), key=lambda j: (-min(j, n - j), j))


def reduce_events(plan, total, inbox_a, inbox_b, piece, ssem, rsem, base, per_chunk, hop):
    order = far_first(plan.nb)

    def ring(n, me, chunks, source, inbox, device, base):
        half = n // 2

        def index(d, step, j):
            return base + (d * half + step - 1) * len(chunks) + chunks.index(j)

        def landing(d, step, j, part):
            offset, size = plan.span(part)
            slot = (d * half + step - 1) * len(chunks) + chunks.index(j)
            return inbox.at[slot, pl.ds(offset, size), :]

        def copy(d, step, j):
            sign = 1 - 2 * d
            part = d if step == 1 else None
            if step == 1:
                src = total.at[source(wrap(me - sign * half, n), j, part), :]
            else:
                src = landing(d, step - 1, j, part)
            i = index(d, step, j)
            return remote(src, landing(d, step, j, part), ssem.at[i], rsem.at[i], device(wrap(me - sign, n)))

        def send(j):
            for d in (0, 1):
                copy(d, 1, j).start()

        def receive(d, step, j):
            sign = 1 - 2 * d
            copy(d, step, j).wait_recv()
            if step < half:
                dest = wrap(me - sign * (half - step), n)
                for part in (0, 1):
                    here = landing(d, step, j, part)
                    own = total[source(dest, j, part), :]
                    here[...] = own if step == 1 and part != d else here[...] + own
                copy(d, step + 1, j).start()
            else:
                part = d if step == 1 else None
                own = source(me, j, part)
                total[own, :] = total[own, :] + landing(d, step, j, part)[...]

        def end():
            for step in range(1, half + 1):
                for j in chunks:
                    for d in (0, 1):
                        copy(d, step, j).wait_send()

        return send, receive, end

    na, nb = plan.na, plan.nb
    send_a, receive_a, end_a = ring(
        na, plan.me_a, order,
        lambda dest, j, part: plan.at(dest, wrap(plan.me_b + j, nb), piece, part),
        inbox_a, lambda a: plan.device(a, plan.me_b), base,
    )
    send_b, receive_b, end_b = ring(
        nb, plan.me_b, [0],
        lambda dest, j, part: plan.at(plan.me_a, dest, piece, part),
        inbox_b, lambda b: plan.device(plan.me_a, b), base + na * nb,
    )
    events = []
    ready = {}
    for pos, j in enumerate(order):
        events.append((0.0 if pos == 0 else max(0.1, per_chunk * (pos - 1)), functools.partial(send_a, j)))
        for step in range(1, plan.half_a + 1):
            at = per_chunk * pos + hop * step
            for d in (0, 1):
                events.append((at + 0.01 * d, functools.partial(receive_a, d, step, j)))
        ready[min(j, nb - j)] = per_chunk * pos + hop * plan.half_a + 0.1
    events.append((ready[plan.half_b], functools.partial(send_b, 0)))
    at = ready[plan.half_b]
    for step in range(1, plan.half_b + 1):
        at = max(at + hop, ready[plan.half_b - step] + 0.1)
        for d in (0, 1):
            events.append((at + 0.01 * d, functools.partial(receive_b, d, step, 0)))

    def end():
        end_a()
        end_b()

    return events, end


def rows_of(tile, k):
    return jnp.broadcast_to(tile[k : k + 1, :], tile.shape)


def columns_of(tile, k):
    return jnp.broadcast_to(tile[:, k : k + 1], tile.shape)


def inverse_factor(block):
    count = BLOCK // 8
    d = [block[8 * i : 8 * i + 8, :] for i in range(count)]
    row = lax.broadcasted_iota(jnp.int32, (8, BLOCK), 0)
    lane = lax.broadcasted_iota(jnp.int32, (8, BLOCK), 1)
    e = [(row + 8 * i == lane).astype(F32) for i in range(count)]
    out = []
    for s in range(count):
        c = [[columns_of(d[i], 8 * s + k) for k in range(8)] for i in range(s, count)]
        pivots = jnp.zeros((8, BLOCK), F32)
        for k in range(8):
            pivot = rows_of(c[0][k], k)
            inverse = 1.0 / pivot
            pivots = jnp.where(row == k, pivot, pivots)
            d_row, e_row = rows_of(d[s], k), rows_of(e[s], k)
            later = [rows_of(c[0][q], k) for q in range(k + 1, 8)]
            for i in range(s, count):
                factor = c[i - s][k] * inverse
                if i == s:
                    factor = jnp.where(row > k, factor, 0.0)
                d[i] = d[i] - factor * d_row
                e[i] = e[i] - factor * e_row
                for q in range(k + 1, 8):
                    c[i - s][q] = c[i - s][q] - factor * later[q - k - 1]
        out.append(e[s] * lax.rsqrt(pivots))
        if s % 2:
            yield 0.072 * (17 - s) * FACTOR_SCALE
    return jnp.concatenate(out, axis=0)


def factor_steps(a, w):
    size = a.shape[0]
    w[...] = jnp.zeros((size, size), F32)
    for o in range(0, size, BLOCK):
        end = o + BLOCK
        inverse = yield from inverse_factor(a[o:end, o:end])
        w[o:end, o:end] = inverse
        if end < size:
            low = exact_dot(a[end:, o:end], inverse, 1, 1)
            a[end:, o:end] = low
            a[end:, end:] = a[end:, end:] - exact_dot(low, low, 1, 1)
        yield 0.5 * FACTOR_SCALE
        if o:
            through = exact_dot(a[o:end, :o], w[:o, :o], 1, 0)
            w[o:end, :o] = -exact_dot(inverse, through, 1, 0)
        yield 0.3 * FACTOR_SCALE


class Mail:
    def __init__(self, send, recv):
        self.send, self.recv, self.used, self.sent = send, recv, 0, []

    def take(self, count):
        self.used += count
        return self.used - count

    def start(self, src, dst, index, device):
        copy = remote(src, dst, self.send.at[index], self.recv.at[index], device)
        copy.start()
        self.sent.append(copy)

    def wait(self, ref, index, device):
        remote(ref, ref, self.send.at[index], self.recv.at[index], device).wait_recv()

    def end(self):
        for copy in self.sent:
            copy.wait_send()


def left_sum(place, mail, partial, inbox, left):
    nx = place.nx
    part = partial.shape[0] // nx
    peers = place.x_peers()
    at = lambda x: pl.ds(pl.multiple_of(x * part, 8), part)
    base = mail.take(nx)
    for o, peer in enumerate(peers, 1):
        mail.start(partial.at[at(wrap(place.x + o, nx)), :], inbox.at[o], base + o, peer)
    total = partial[at(place.x), :]
    for o, peer in enumerate(peers, 1):
        mail.wait(inbox.at[o], base + o, peer)
        total = total + inbox[o]
    left[at(place.x), :] = total
    base = mail.take(nx)
    for o, peer in enumerate(peers, 1):
        mail.start(left.at[at(place.x), :], left.at[at(place.x), :], base + o, peer)
    for o, peer in enumerate(peers, 1):
        mail.wait(left.at[at(wrap(place.x - o, nx)), :], base + o, peer)


def gram_steps(place, mail, left, both, part, z_in, y_in, gram, meanwhile):
    core, partner = place.core, place.partner()
    nz, ny, nx = place.nz, place.ny, place.nx
    half = left.shape[1]
    across = 2 * half // nx
    rows = across // nz

    i = mail.take(1)
    mail.start(left, both.at[core], i, partner)
    both[core] = left[...]
    mail.wait(both.at[1 - core], i, partner)
    per = half // across
    lanes = pl.ds(pl.multiple_of(lax.rem(place.x, per) * across, BLOCK), across)
    part[...] = exact_dot(both[lax.div(place.x, per), :, lanes], left[...], 0, 0)

    z_peers, y_peers, x_peers = place.z_peers(), place.y_peers(), place.x_peers()
    at_z = lambda z: pl.ds(pl.multiple_of(z * rows, 8), rows)
    i = mail.take(nz)
    for o, peer in enumerate(z_peers, 1):
        mail.start(part.at[at_z(wrap(place.z + o, nz)), :], z_in.at[o], i + o, peer)
    meanwhile()
    yield GRAM_TIMES[0]
    total = part[at_z(place.z), :]
    for o, peer in enumerate(z_peers, 1):
        mail.wait(z_in.at[o], i + o, peer)
        total = total + z_in[o]
    i = mail.take(ny)
    y_in[place.y] = total
    for o, peer in enumerate(y_peers, 1):
        mail.start(y_in.at[place.y], y_in.at[place.y], i + o, peer)
    yield GRAM_TIMES[1]
    for o, peer in enumerate(y_peers, 1):
        mail.wait(y_in.at[wrap(place.y - o, ny)], i + o, peer)
    total = y_in[0]
    for y in range(1, ny):
        total = total + y_in[y]

    def at(x, z):
        return gram.at[core, pl.ds(pl.multiple_of(x * across + z * rows, 8), rows), :]

    at(place.x, place.z)[...] = total
    i = mail.take(nz)
    for o, peer in enumerate(z_peers, 1):
        mail.start(at(place.x, place.z), at(place.x, place.z), i + o, peer)
    yield GRAM_TIMES[2]
    for o, peer in enumerate(z_peers, 1):
        mail.wait(at(place.x, wrap(place.z - o, nz)), i + o, peer)
    whole = lambda x: gram.at[core, pl.ds(pl.multiple_of(x * across, 8), across), :]
    i = mail.take(nx)
    for o, peer in enumerate(x_peers, 1):
        mail.start(whole(place.x), whole(place.x), i + o, peer)
    yield GRAM_TIMES[3]
    for o, peer in enumerate(x_peers, 1):
        mail.wait(whole(wrap(place.x - o, nx)), i + o, peer)
    i = mail.take(1)
    mail.start(gram.at[core], gram.at[core], i, partner)
    yield GRAM_TIMES[4]
    mail.wait(gram.at[1 - core], i, partner)


def split_terms(left):
    upper = left[...].astype(BF16)
    lower = (left[...] - upper.astype(F32)).astype(BF16)
    return jnp.concatenate([upper, lower], axis=1)


def project(pair, terms, total, begin, size):
    rows = pair.shape[1]
    half = total.shape[1]
    width = 512 if size >= 512 else BLOCK

    def block(start, width):
        at = pl.ds(pl.multiple_of(start, BLOCK), width)
        value = sum(
            lax.dot_general(pair[c, :, at], terms[c * rows : (c + 1) * rows, :], (((0,), (0,)), ((), ())),
                            preferred_element_type=F32)
            for c in range(2)
        )
        total[at, :] = value[:, :half] + value[:, half:]

    pl.loop(0, size // width)(lambda i: block(begin + i * width, width))
    if size % width:
        block(begin + size // width * width, size % width)


def merge(steps, events, begin=0.0):
    events = sorted(events, key=lambda e: e[0])
    now = begin
    for spent in steps:
        now += spent
        while events and events[0][0] <= now:
            events.pop(0)[1]()
    for _, action in events:
        action()


def step_kernel(dims, magnitude, momentum, gradient, prior, gathered, stacked, right_next,
                mom, grad, pair, mine, given, buf, partial, x_in, left, both, part, z_in, y_in, gram,
                a, w, total, terms, in_yz, in_z, in_zy, in_y, pieces, ortho, nz_in, ny_in, nx_in,
                load_sem, one_send, one_recv, two_send, two_recv, sum_send, sum_recv,
                swap_send, swap_recv, send, recv):
    place = Place(*dims)
    nz, ny, nx = dims
    core, partner = place.core, place.partner()
    shard, rank = prior.shape
    half = rank // 2
    rows, columns = mom.shape
    piece = 2 * shard
    long = 128 if piece == 208 else 32
    loads = [pltpu.make_async_copy(momentum, mom, load_sem.at[0]), pltpu.make_async_copy(gradient, grad, load_sem.at[1])]
    for load in loads:
        load.start()
    greet([partner] + place.x_peers() + place.y_peers() + place.z_peers())
    mail = Mail(send, recv)

    low, high = prior[:, :half].astype(F32), prior[:, half:].astype(F32)
    given[...] = jnp.where(core == 0, high, low)
    at_mine = mine.at[pl.ds(pl.multiple_of(core * shard, 8), shard), :]
    at_theirs = mine.at[pl.ds(pl.multiple_of((1 - core) * shard, 8), shard), :]
    i = mail.take(1)
    mail.start(given, at_mine, i, partner)
    at_mine[...] = jnp.where(core == 0, low, high)
    mail.wait(at_theirs, i, partner)
    at_chip = lambda slot: pl.ds(pl.multiple_of(slot * piece, 16), piece)
    buf[at_chip(place.chip()), :] = mine[...].astype(BF16)
    swap_blend = mail.take(1)

    def blend():
        for load in loads:
            load.wait()
        width = 512 if columns % 512 == 0 else BLOCK

        @pl.loop(0, columns // width)
        def _(i):
            at = pl.ds(pl.multiple_of(i * width, BLOCK), width)
            pair[core, :, at] = (mom[:, at] + grad[:, at].astype(F32)).astype(BF16)

        mail.start(pair.at[core], pair.at[core], swap_blend, partner)

    plans = lambda unit: (Plan(place, True, 0, long, unit), Plan(place, False, long, piece - long, unit))
    gather_plane(buf, piece, plans(16), one_send, one_recv, lambda *_: None, [(0.5, blend)])
    mail.wait(pair.at[1 - core], swap_blend, partner)

    width = 1664 if columns % 1664 == 0 else BLOCK
    partial[...] = jnp.zeros_like(partial)

    @pl.loop(0, columns // width)
    def _(i):
        at = pl.ds(pl.multiple_of(i * width, BLOCK), width)
        for c in range(2):
            own = slice(c * rows, (c + 1) * rows)
            partial[own, :] += jnp.dot(pair[c, :, at], buf[at, :], preferred_element_type=F32)

    left_sum(place, mail, partial, x_in, left)

    sum_long = SUM_LONG if piece == 208 else 32
    bulk_y = Plan(place, False, 0, sum_long, 8)
    bulk_z = Plan(place, True, sum_long, piece - sum_long, 8)
    events_y, end_y = reduce_events(bulk_y, total, in_yz, in_z, piece, sum_send, sum_recv, 0, PER_Y, HOP_Y)
    events_z, end_z = reduce_events(bulk_z, total, in_zy, in_y, piece, sum_send, sum_recv, nz * ny + nz, PER_Z, HOP_Z)

    terms[...] = split_terms(left)
    parts = nz // 2
    size = columns // parts

    def project_part(ahead):
        start = wrap(lax.div(place.z, 2) + ahead, parts) * size
        project(pair, terms, total, start, size)

    first = parts // 2
    others = sorted((k for k in range(parts) if k != first), key=lambda k: (-min(k, parts - k), k))
    events_part = [(0.05, functools.partial(project_part, k)) for k in others]

    def chain():
        yield from gram_steps(place, mail, left, both, part, z_in, y_in, gram, lambda: project_part(first))
        for c in range(2):
            a[:, c * half : (c + 1) * half] = gram[c]
        yield from factor_steps(a, w)
        own = pl.ds(pl.multiple_of(core * rows, 8), rows)
        ortho[...] = exact_dot(both[0, own, :], w[:, :half], 1, 1) + exact_dot(both[1, own, :], w[:, half:], 1, 1)
        yield 1.0

    merge(chain(), events_y + events_z + events_part)

    own = pl.ds(pl.multiple_of(place.chip() * piece, 8), piece)
    i = mail.take(1)
    mail.start(total.at[own, :], pieces.at[core], i, partner)
    pieces[core] = total[own, :]
    mail.wait(pieces.at[1 - core], i, partner)
    value = exact_dot(pieces[0], w[:, :half], 1, 1) + exact_dot(pieces[1], w[:, half:], 1, 1)
    squares = jnp.broadcast_to(jnp.sum(value * value, axis=0, keepdims=True), (8, rank))
    right = jnp.where(core == 0, value[:shard], value[shard:])
    share = gathered.at[core]
    share[at_chip(place.chip()), :] = jnp.where(core == 0, value[:, :half], value[:, half:]).astype(BF16)

    def level(inbox, me, peers, count):
        return inbox, me, peers, count, mail.take(count)

    def level_start(inbox, me, peers, count, base, value):
        inbox[me] = value
        for o, peer in enumerate(peers, 1):
            mail.start(inbox.at[me], inbox.at[me], base + o, peer)

    def level_done(inbox, me, peers, count, base):
        for o, peer in enumerate(peers, 1):
            mail.wait(inbox.at[wrap(me - o, count)], base + o, peer)
        total = inbox[0]
        for i in range(1, count):
            total = total + inbox[i]
        return total

    z_level = level(nz_in, place.z, place.z_peers(), nz)
    y_level = level(ny_in, place.y, place.y_peers(), ny)
    x_level = level(nx_in, place.x, place.x_peers(), nx)
    level_start(*z_level, squares)

    def finish():
        column_scale = 1.0 / jnp.sqrt(level_done(*x_level)[:1] + 1e-06)
        right_next[...] = (right * column_scale).astype(BF16)
        stacked[:rows, :] = ortho[...].astype(BF16)
        stacked[rows:, :] = (ortho[...] * column_scale * magnitude).astype(BF16)

    def forward(plan, a, b):
        offset = 0 if plan.offset == 0 else nz * ny
        here = share.at[plan.at(a, b, piece), :]
        slot = offset + plan.slot(a, b)
        remote(here, here, swap_send.at[slot], swap_recv.at[slot], partner).start()

    gather_plane(share, piece, plans(16), two_send, two_recv, forward, [
        (1.2, lambda: level_start(*y_level, level_done(*z_level))),
        (2.0, lambda: level_start(*x_level, level_done(*y_level))),
        (3.0, finish),
    ])
    for offset, size, base in ((0, long, 0), (long, piece - long, nz * ny)):
        for slot in range(nz * ny):
            at = slice(slot * piece + offset, slot * piece + offset + size)
            there, here = gathered.at[1 - core, at, :], gathered.at[core, at, :]
            remote(there, there, swap_send.at[base + slot], swap_recv.at[base + slot], partner).wait_recv()
            remote(here, here, swap_send.at[base + slot], swap_recv.at[base + slot], partner).wait_send()
    end_y()
    end_z()
    mail.end()


def step_call(dims, magnitude, momentum, gradient, prior):
    nz, ny, nx = dims
    shard, rank = prior.shape
    rows, columns = momentum.shape
    half = rank // 2
    piece = 2 * shard
    long = 128 if piece == 208 else 32
    sum_long = SUM_LONG if piece == 208 else 32
    chips = nz * ny
    across = rank // nx
    ring = 2 * chips + nz + ny
    mails = 5 + 4 * nx + 3 * nz + 2 * ny
    dma = pltpu.SemaphoreType.DMA
    vmem = pltpu.VMEM
    return pl.pallas_call(
        functools.partial(step_kernel, dims, magnitude),
        out_shape=(
            jax.ShapeDtypeStruct((2, columns, half), BF16),
            jax.ShapeDtypeStruct((2 * rows, rank), BF16),
            jax.ShapeDtypeStruct((shard, rank), BF16),
        ),
        in_specs=[pl.BlockSpec(memory_space=pl.ANY)] * 2 + [VMEM_SPEC],
        out_specs=(VMEM_SPEC,) * 3,
        scratch_shapes=[
            vmem((rows, columns), F32), vmem((rows, columns), BF16),
            vmem((2, rows, columns), BF16),
            vmem((piece, half), F32), vmem((shard, half), F32), vmem((columns, half), BF16),
            vmem((2 * rows, half), F32), vmem((nx, 2 * rows // nx, half), F32), vmem((2 * rows, half), F32),
            vmem((2, 2 * rows, half), F32), vmem((across, half), F32),
            vmem((nz, across // nz, half), F32), vmem((ny, across // nz, half), F32),
            vmem((2, rank, half), F32), vmem((rank, rank), F32), vmem((rank, rank), F32),
            vmem((columns, half), F32), vmem((2 * rows, rank), BF16),
            vmem((chips, sum_long, half), F32), vmem((nz, sum_long, half), F32),
            vmem((chips, piece - sum_long, half), F32), vmem((ny, piece - sum_long, half), F32),
            vmem((2, piece, half), F32), vmem((rows, rank), F32),
            vmem((nz, 8, rank), F32), vmem((ny, 8, rank), F32), vmem((nx, 8, rank), F32),
            dma((2,)), dma((ring,)), dma((ring,)), dma((ring,)), dma((ring,)), dma((ring,)), dma((ring,)),
            dma((2 * chips,)), dma((2 * chips,)), dma((mails,)), dma((mails,)),
        ],
        compiler_params=pltpu.CompilerParams(
            collective_id=0, has_side_effects=True, vmem_limit_bytes=VMEM_LIMIT
        ),
        name="dion_step",
    )(momentum, gradient, prior)


def apply_kernel(step, momentum, gradient, stacked, gathered, momentum_next, update):
    half = gathered.shape[2]
    rows = momentum.shape[0]
    dims = (((1,), (1,)), ((), ()))
    products = sum(
        lax.dot_general(stacked[:, c * half : (c + 1) * half], gathered[c], dims, preferred_element_type=F32)
        for c in range(2)
    )
    blended = momentum[...] + gradient[...].astype(F32)
    momentum_next[...] = blended - step * products[:rows]
    update[...] = products[rows:].astype(BF16)


def apply_call(step, momentum, gradient, stacked, gathered):
    rows, columns = momentum.shape
    rank = stacked.shape[1]
    width = columns // 2 if columns % 256 == 0 else BLOCK
    tile = pl.BlockSpec((rows, width), lambda i: (0, i))
    return pl.pallas_call(
        functools.partial(apply_kernel, step),
        grid=(columns // width,),
        out_shape=(
            jax.ShapeDtypeStruct((rows, columns), F32),
            jax.ShapeDtypeStruct((rows, columns), BF16),
        ),
        in_specs=[
            tile, tile, pl.BlockSpec(stacked.shape, lambda i: (0, 0)),
            pl.BlockSpec((2, width, rank // 2), lambda i: (0, i, 0)),
        ],
        out_specs=(tile, tile),
        compiler_params=pltpu.CompilerParams(vmem_limit_bytes=VMEM_LIMIT),
        name="apply",
    )(momentum, gradient, stacked, gathered)


def local(dims, momentum, gradient, right_prior):
    decay = 0.95
    prior = right_prior[0]
    rows_all = momentum.shape[0] * lax.axis_size("fsdp")
    cols_all = momentum.shape[1] * lax.axis_size("tp")
    magnitude = math.sqrt(rows_all * cols_all / prior.shape[1])
    gathered, stacked, right_next = step_call(dims, magnitude, momentum, gradient, prior)
    momentum_next, update = apply_call(1.0 - decay, momentum, gradient, stacked, gathered)
    return (momentum_next, update, right_next[None])


def solution(mesh):
    fsdp, tp = mesh.shape["fsdp"], mesh.shape["tp"]
    dims = (fsdp // (2 * Y_CHIPS), Y_CHIPS, tp)
    in_specs = (P("fsdp", "tp"), P("fsdp", "tp"), P("tp", "fsdp", None))
    out_specs = (P("fsdp", "tp"), P("fsdp", "tp"), P("tp", "fsdp", None))
    return jax.shard_map(
        functools.partial(local, dims), mesh=mesh, in_specs=in_specs, out_specs=out_specs, check_vma=False
    )
```
